128 devices in a mesh: region: 4 (over x_lo, core), subj: 32 (over y, z, x_hi).
Axes of the slice: x: 4 (x_hi: 2, x_lo: 2; x = x_hi * 2 + x_lo), y: 4, z: 4, core: 2. Of those that a mesh axis runs over, the one named last changes fastest.
Arguments:
- coords: float32 [8192, 3, 2048], P('subj', None, 'region'), may hold values from -30 to 30
- transform: float32 [8192, 3, 3], P('subj'), may hold values from -3.5 to 3.5
- labels: int32 [2048, 1], P('region'), may hold values from 0 to 3; in each aligned block of 512 rows (0 to 511, 512 to 1023, ...) at most 256 rows name the same one
- subject_order: int32 [8192], replicated, may hold values from 0 to 8191, each once
Outputs:
- region_gram: float32 [4, 8192, 8192], P('region', 'subj')
The draws below stay inside these ranges and needn't reach their ends.
Inputs may be any that keep to these rules, and one draw needn't show every extreme that they name: `labels`: among the 512 vertices of one device no region label occurs more than 256 times, and some label reaches 256. `subject_order`: a permutation of the subjects.
All inputs are finite; a program needn't handle non-finite values.
Results may differ from the reference program's by a relative error of at most 0.0012.
Values may be sent and summed in bfloat16 or wider, within the bound.
A program may use at most 128 MiB of HBM per device.

```python
import math
import jax
import jax.numpy as jnp
import numpy as np
from jax import lax

SUBJECTS = 8192
V_DEV = 512
CAP = 256
VERTS = 2048
REGIONS = 4


def draw_coords(key, part):
    key_offset, key_shift, key_noise = jax.random.split(key, 3)
    position = jnp.arange(VERTS, dtype=jnp.float32) / VERTS
    offset = jax.random.uniform(key_offset, (1, 3, 1), jnp.float32, 1.0, 2.5)
    shift = 1.5 * jax.random.normal(key_shift, (SUBJECTS, 3, 1), jnp.float32)
    noise = 2.5 * jax.random.normal(key_noise, (SUBJECTS, 3, VERTS), jnp.float32)
    values = offset * (1.0 + 2.0 * position)[None, None, :] + shift + noise
    return jnp.clip(values, -30.0, 30.0).astype(jnp.float32)


def steps_of(rng, shape, shards, smallest, largest):
    factor_of = 1.0
    for dim, shards_of in shards:
        steps = jax.random.uniform(jax.random.fold_in(jax.random.fold_in(rng, 6), dim), (shards_of,), jnp.float32, smallest / len(shards), largest / len(shards))
        factor_of = factor_of * jnp.repeat(jnp.exp(steps), shape[dim] // shards_of).reshape((-1,) + (1,) * (len(shape) - 1 - dim))
    return factor_of


def assign_block(stream_key, own, number, rows, amount, top, reach, lean):
    ranking = jax.random.permutation(stream_key, amount)
    packed, common = portions_of(amount, rows * top, reach, lean, True), portions_of(amount, rows * top, reach, lean, False)
    places = jnp.arange(amount)

    def named(lengths, turn):
        used = int((lengths > 0).sum())
        fixed = max(1, used // 4)
        moved = fixed + (places - fixed + turn * (used - fixed)) % max(1, amount - fixed)
        return jnp.zeros((amount,), jnp.int32).at[ranking[jnp.where(places < fixed, places, moved)]].set(jnp.asarray(lengths, jnp.int32))

    lengths = jnp.where(number % 4 == 0, named(packed, number // 4), named(common, number - number // 4 - 1))
    mixed = jax.random.permutation(jax.random.fold_in(own, 3), amount)
    donor, receiver = mixed[0:amount // 2 * 2:2], mixed[1:amount // 2 * 2:2]
    slack = jnp.minimum(lengths[donor] - 1, reach - lengths[receiver]) // 2
    slack = jnp.where((donor == ranking[0]) | (receiver == ranking[0]) | (lengths[receiver] == 0), 0, jnp.maximum(slack, 0))
    moved = jax.random.randint(jax.random.fold_in(own, 4), (amount // 2,), 0, 1 << 20) % (slack + 1)
    lengths = lengths.at[donor].add(-moved).at[receiver].add(moved)
    items = jnp.searchsorted(jnp.cumsum(lengths), jnp.arange(rows * top), side="right").astype(jnp.int32)
    listing = items.reshape(top, rows).T
    listing = listing[jax.random.permutation(jax.random.fold_in(own, 1), rows)]
    turn = jax.random.randint(jax.random.fold_in(own, 2), (rows, 1), 0, top)
    return jnp.take_along_axis(listing, (jnp.arange(top)[None, :] + turn) % top, axis=1)


def portions_of(number_of, total, reach, skew, full):
    weights = [(1 << 20) // math.isqrt(grade ** skew) + 1 for grade in range(1, number_of + 1)]
    largest = reach if full else min(reach, max(-(-total // number_of), total * weights[0] // sum(weights)))
    least = 1 if total - largest >= number_of - 1 else 0
    counts, surplus = [largest] + [least] * (number_of - 1), total - largest - least * (number_of - 1)
    while surplus > 0:
        movable = [i for i in range(1, number_of) if counts[i] < largest] or [i for i in range(1, number_of) if counts[i] < reach]
        mass, left = sum([weights[i] for i in movable]), surplus
        for i in movable:
            more = min(reach - counts[i], max(1, left * weights[i] // mass), surplus)
            counts[i] = counts[i] + more
            surplus = surplus - more
    return np.array(counts)


def gaussian(stream_key, shape, width, limit, cuts=(), kind=jnp.bfloat16):
    drawn = width * jax.random.normal(stream_key, shape, jnp.float32)
    if cuts:
        drawn = drawn * steps_of(stream_key, shape, cuts, -0.22, 0.18)
    return jnp.clip(drawn, -limit, limit).astype(kind)


def setup_inputs(seed: int = 0) -> dict:
    seeds = jax.random.split(jax.random.key(seed), 5)
    coords = draw_coords(jax.random.fold_in(seeds[4], 71), 0)
    transform = gaussian(seeds[1], (SUBJECTS, 3, 3), 3 ** -0.5, 3.5, ((0, 32),), jnp.float32)
    labels_keys = jax.random.split(jax.random.fold_in(seeds[2], 1), VERTS // V_DEV)
    labels_turns = jax.random.permutation(jax.random.fold_in(seeds[2], 3), VERTS // V_DEV)
    labels = jax.vmap(lambda own, number: assign_block(jax.random.fold_in(seeds[2], 2), own, number, V_DEV, REGIONS, 1, CAP, 2))(labels_keys, labels_turns).reshape((VERTS, 1))
    subject_order = jax.random.permutation(seeds[3], SUBJECTS).astype(jnp.int32)
    return dict(coords=coords, transform=transform, labels=labels, subject_order=subject_order)


def reference(coords, transform, labels, subject_order):
    moved = (transform[:, :, 0:1] * coords[:, 0:1, :]
             + transform[:, :, 1:2] * coords[:, 1:2, :]
             + transform[:, :, 2:3] * coords[:, 2:3, :])
    centroid = jnp.sum(moved, axis=2, keepdims=True) / VERTS
    centered = (moved - centroid).astype(jnp.bfloat16)
    flat = centered.reshape(SUBJECTS, 3 * VERTS)
    label_row = labels[:, 0]
    scale = 1.0 / (3.0 * VERTS)

    def one_region(region_id):
        keep = (label_row == region_id)[None, None, :]
        masked = jnp.where(keep, centered, jnp.zeros_like(centered)).reshape(SUBJECTS, 3 * VERTS)
        gram = lax.dot_general(masked, flat, (((1,), (1,)), ((), ())), preferred_element_type=jnp.float32)
        gram = gram * scale
        return jnp.take(gram, subject_order, axis=1)

    return lax.map(one_region, jnp.arange(REGIONS, dtype=jnp.int32))
```

```python
import functools

import jax
import jax.numpy as jnp
from jax import lax
from jax.experimental import pallas as pl
from jax.experimental.pallas import tpu as pltpu
from jax.sharding import PartitionSpec as P

CAP = 256
B = 256
G = 4
F = 3 * CAP
MESH = pl.DeviceIdType.MESH
NT = (((1,), (1,)), ((), ()))


def dev(l, c, y, z, u):
    return (2 * l + c, 8 * lax.rem(y, 4) + 2 * lax.rem(z, 4) + u)


def gram_kernel(cent, tgt, out, snd, panels, res, relay_ss, relay_rs, ring_ss, ring_rs, sib_ss, sib_rs, res_ss, res_rs):
    r, s = lax.axis_index("region"), lax.axis_index("subj")
    l, c = r // 2, lax.rem(r, 2)
    y, z, u = s // 8, lax.rem(s // 2, 4), lax.rem(s, 2)
    barrier = pltpu.get_barrier_semaphore()
    own = c == u

    def copy(src, dst, ss, rs, to):
        return pltpu.make_async_remote_copy(
            src_ref=src, dst_ref=dst, send_sem=ss, recv_sem=rs, device_id=to, device_id_type=MESH
        )

    for k in range(1, 8):
        q = lax.rem(l * 4 + c * 2 + u + k, 8)
        pl.semaphore_signal(barrier, inc=1, device_id=dev(q // 4, lax.rem(q // 2, 2), y, z, lax.rem(q, 2)), device_id_type=MESH)
    for k in range(1, 4):
        for cc in range(2):
            for uu in range(2):
                pl.semaphore_signal(barrier, inc=1, device_id=dev(l, cc, y + k, z, uu), device_id_type=MESH)
                pl.semaphore_signal(barrier, inc=1, device_id=dev(l, cc, y, z + k, uu), device_id_type=MESH)
    pl.semaphore_wait(barrier, 31)

    row = tgt[0:1, :]
    for region in range(G):
        lr, ur = region // 2, region % 2
        slots = lax.broadcasted_iota(jnp.int32, (CAP, row.shape[1]), 0) + region * CAP
        pick = jnp.where(slots == row, 1.0, 0.0).astype(jnp.bfloat16)
        for d in range(3):
            snd[region, :, d * CAP : (d + 1) * CAP] = lax.dot_general(
                cent[d], pick, NT, preferred_element_type=jnp.float32
            ).astype(jnp.bfloat16)
        mine = jnp.logical_and(own, jnp.logical_and(l == lr, u == ur))

        @pl.when(mine)
        def _():
            pltpu.make_async_copy(snd.at[region], panels.at[0, r], relay_rs.at[r]).start()

        @pl.when(jnp.logical_not(mine))
        def _():
            copy(snd.at[region], panels.at[0, r], relay_ss.at[region], relay_rs.at[r], dev(lr, u, y, z, ur)).start()

    sibling = dev(l, 1 - c, y, z, u)
    yp, ym = dev(l, c, y + 1, z, u), dev(l, c, y + 3, z, u)
    zp, zm = dev(l, c, y, z + 1, u), dev(l, c, y, z + 3, u)

    def send(kind, src, dst, g, to):
        return copy(panels.at[src, g], panels.at[dst, g], ring_ss.at[kind, g], ring_rs.at[kind, g], to)

    def share(slot, g):
        return copy(panels.at[2 * slot, g], panels.at[2 * slot + 1, g], sib_ss.at[slot, g], sib_rs.at[slot, g], sibling)

    for g in range(G):
        copy(snd.at[0], panels.at[0, g], relay_ss.at[0], relay_rs.at[g], sibling).wait_recv()
        send(0, 0, 6, g, yp).start()
        send(1, 0, 2, g, ym).start()
        send(2, 0, 10, g, zp).start()
        send(3, 0, 8, g, zm).start()
        share(0, g).start()

    def block(bi, ai, rows=B, at=0):
        total = None
        for g in range(G):
            part = lax.dot_general(
                panels[bi, g, at : at + rows, :], panels[ai, g], NT, preferred_element_type=jnp.float32
            )
            total = part if total is None else total + part
        return total * (1.0 / (3.0 * 2048))

    def number(yb, zb, hb):
        return 8 * lax.rem(yb, 4) + 2 * lax.rem(zb, 4) + hb

    sent = []

    def deliver(t, bi, ai, b, owner, maybe_self=False, half=None):
        if half is None:
            res[t] = block(bi, ai)
            src, dst, sem = res.at[t], out.at[b], res_rs.at[b]
        else:
            part = pl.ds(half * 128, 128)
            res[t, part, :] = block(bi, ai, 128, half * 128)
            src, dst = res.at[t, part], out.at[b, part]
            sem = res_rs.at[b] if half == 0 else res_rs.at[32 + lax.rem(b, 2)]
        remote = copy(src, dst, res_ss.at[t], sem, owner)
        if maybe_self:

            @pl.when(own)
            def _():
                pltpu.make_async_copy(src, dst, sem).start()

            @pl.when(jnp.logical_not(own))
            def _():
                remote.start()
        else:
            remote.start()
        sent.append((remote, maybe_self))

    def cols(dz):
        return 0 if dz == 0 else 7 + dz

    def head(j):
        return c if j == 0 else 1 - c

    def home_rows(t, dz):
        for j in range(2):
            deliver(t + j, cols(dz), j, number(y, z + dz, c), dev(l, u, y, z, head(j)), maybe_self=j == 0)

    def home_cols(t, dy):
        for j in range(2):
            deliver(t + j, 2 * dy + j, 0, number(y + dy, z, head(j)), dev(l, u, y, z, c), maybe_self=True)

    def by_y(t, dy, dz, half=None):
        for j in range(2):
            deliver(t + j, cols(dz), 2 * dy + j, number(y, z + dz, c), dev(l, u, y + dy, z, head(j)), half=half)

    def by_z(t, dy, dz, half=None):
        for j in range(2):
            deliver(t + j, 2 * dy + j, cols(dz), number(y + dy, z, head(j)), dev(l, u, y, z + dz, c), half=half)

    def got_share(slot):
        for g in range(G):
            share(slot, g).wait_recv()

    got_share(0)
    home_rows(0, 0)
    for g in range(G):
        send(0, 0, 6, g, yp).wait_recv()
        if g < 2:
            copy(panels.at[6, g], panels.at[4, g], ring_ss.at[4, g], ring_rs.at[4, g], yp).start()
        share(3, g).start()
        send(2, 0, 10, g, zp).wait_recv()
        if g < 2:
            copy(panels.at[10, g], panels.at[9, g], ring_ss.at[5, g], ring_rs.at[5, g], zp).start()
        send(1, 0, 2, g, ym).wait_recv()
        if g >= 2:
            copy(panels.at[2, g], panels.at[4, g], ring_ss.at[4, g], ring_rs.at[4, g], ym).start()
        share(1, g).start()
        send(3, 0, 8, g, zm).wait_recv()
        if g >= 2:
            copy(panels.at[8, g], panels.at[9, g], ring_ss.at[5, g], ring_rs.at[5, g], zm).start()
    got_share(1)
    got_share(3)
    home_rows(2, 1)
    home_rows(4, 3)
    home_cols(6, 1)
    home_cols(8, 3)
    by_y(10, 3, 1)
    by_y(12, 1, 3)
    by_z(14, 1, 1)
    by_z(16, 3, 3)
    for g in range(G):
        copy(panels.at[6, g], panels.at[4, g], ring_ss.at[4, g], ring_rs.at[4, g], yp).wait_recv()
        share(2, g).start()
    for g in range(G):
        copy(panels.at[10, g], panels.at[9, g], ring_ss.at[5, g], ring_rs.at[5, g], zp).wait_recv()
    home_rows(18, 2)
    by_y(20, 1, 2)
    by_y(22, 3, 2)
    got_share(2)
    home_cols(24, 2)
    by_z(26, 2, 1)
    by_z(28, 2, 3)
    by_y(30, 2, 2, 0)
    by_z(32, 2, 2, 1)

    for region in range(G):
        mine = jnp.logical_and(own, jnp.logical_and(l == region // 2, u == region % 2))

        @pl.when(jnp.logical_not(mine))
        def _():
            copy(snd.at[region], panels.at[0, r], relay_ss.at[region], relay_rs.at[r], sibling).wait_send()

    for kind in range(4):
        for g in range(G):
            send(kind, 0, 2, g, yp).wait_send()
    for kind in (4, 5):
        for g in range(G):
            send(kind, 0, 2, g, yp).wait_send()
    for slot in range(4):
        for g in range(G):
            share(slot, g).wait_send()
    for remote, maybe_self in sent:
        if maybe_self:

            @pl.when(jnp.logical_not(own))
            def _():
                remote.wait_send()
        else:
            remote.wait_send()
    for ey in range(4):
        for ez in range(4):
            for h in range(2):
                b = number(y + ey, z + ez, h)
                if (ey, ez) == (2, 2):
                    for half, sem in ((0, res_rs.at[b]), (1, res_rs.at[32 + h])):
                        part = pl.ds(half * 128, 128)
                        copy(res.at[0, part], out.at[b, part], res_ss.at[0], sem, sibling).wait_recv()
                else:
                    copy(res.at[0], out.at[b], res_ss.at[0], res_rs.at[b], sibling).wait_recv()


def gram(cent, tgt):
    dma = pltpu.SemaphoreType.DMA
    return pl.pallas_call(
        gram_kernel,
        out_shape=jax.ShapeDtypeStruct((32, B, B), jnp.float32),
        in_specs=[pl.BlockSpec(memory_space=pltpu.VMEM)] * 2,
        out_specs=pl.BlockSpec(memory_space=pl.ANY),
        scratch_shapes=[
            pltpu.VMEM((G, B, F), jnp.bfloat16),
            pltpu.VMEM((11, G, B, F), jnp.bfloat16),
            pltpu.VMEM((34, B, B), jnp.float32),
            dma((G,)),
            dma((G,)),
            dma((6, G)),
            dma((6, G)),
            dma((4, G)),
            dma((4, G)),
            dma((34,)),
            dma((34,)),
        ],
        compiler_params=pltpu.CompilerParams(
            collective_id=0, has_side_effects=True, vmem_limit_bytes=50 * 2**20
        ),
        cost_estimate=pl.CostEstimate(flops=13 * 10**9, bytes_accessed=10 * 2**20, transcendentals=0),
        name="gram",
    )(cent, tgt)


W = 512


def order_kernel(order, gt, out, rows):
    step = pl.program_id(0)

    def body(k, _):
        for i in range(8):
            rows[pl.ds(k * 8 + i, 1), :] = gt[pl.ds(order[step * W + k * 8 + i], 1), :]
        return 0

    lax.fori_loop(0, W // 8, body, 0)
    out[0] = rows[...].T


def ordered(order, gt):
    n = gt.shape[0]
    return pl.pallas_call(
        order_kernel,
        out_shape=jax.ShapeDtypeStruct((1, B, n), jnp.float32),
        grid_spec=pltpu.PrefetchScalarGridSpec(
            num_scalar_prefetch=1,
            grid=(n // W,),
            in_specs=[pl.BlockSpec((n, B), lambda i, o: (0, 0), pipeline_mode=pl.Buffered(1))],
            out_specs=pl.BlockSpec((1, B, W), lambda i, o: (0, 0, i)),
            scratch_shapes=[pltpu.VMEM((W, B), jnp.float32)],
        ),
        compiler_params=pltpu.CompilerParams(vmem_limit_bytes=40 * 2**20),
        cost_estimate=pl.CostEstimate(flops=0, bytes_accessed=2 * n * B * 4, transcendentals=0),
        name="ordered",
    )(order, gt)


def local(coords, transform, labels, subject_order):
    verts = coords.shape[2] * lax.axis_size("region")
    moved = jnp.stack(
        [
            transform[:, d, 0:1] * coords[:, 0, :]
            + transform[:, d, 1:2] * coords[:, 1, :]
            + transform[:, d, 2:3] * coords[:, 2, :]
            for d in range(3)
        ]
    )
    totals = lax.psum(jnp.sum(moved, axis=2), "region")
    cent = (moved - (totals / verts)[:, :, None]).astype(jnp.bfloat16)
    lab = labels[:, 0]
    n = lab.shape[0]
    before = jnp.arange(n)[:, None] < jnp.arange(n)[None, :]
    rank = jnp.sum(jnp.where((labels == lab[None, :]) & before, 1, 0), axis=0)
    tgt = jnp.broadcast_to((lab * CAP + rank)[None, :], (8, n))
    gt = gram(cent, tgt)
    return ordered(subject_order, gt.reshape(32 * B, B))


def solution(mesh):
    placed = (P("subj", None, "region"), P("subj", None, None), P("region", None), P())
    return jax.shard_map(
        local, mesh=mesh, in_specs=placed, out_specs=P("region", "subj", None), check_vma=False
    )
```

```python
import functools

import jax
import jax.numpy as jnp
from jax import lax
from jax.experimental import pallas as pl
from jax.experimental.pallas import tpu as pltpu
from jax.sharding import PartitionSpec as P

CAP = 256
B = 256
G = 4
F = 3 * CAP
MESH = pl.DeviceIdType.MESH
NT = (((1,), (1,)), ((), ()))


def dev(l, c, y, z, u):
    return (2 * l + c, 8 * lax.rem(y, 4) + 2 * lax.rem(z, 4) + u)


def gram_kernel(cent, tgt, out, out_scale, snd, panels, scales, res, relay_ss, relay_rs, ring_ss, ring_rs, sib_ss, sib_rs, res_ss, res_rs, scale_ss, scale_rs):
    r, s = lax.axis_index("region"), lax.axis_index("subj")
    l, c = r // 2, lax.rem(r, 2)
    y, z, u = s // 8, lax.rem(s // 2, 4), lax.rem(s, 2)
    barrier = pltpu.get_barrier_semaphore()
    own = c == u

    def copy(src, dst, ss, rs, to):
        return pltpu.make_async_remote_copy(
            src_ref=src, dst_ref=dst, send_sem=ss, recv_sem=rs, device_id=to, device_id_type=MESH
        )

    for k in range(1, 8):
        q = lax.rem(l * 4 + c * 2 + u + k, 8)
        pl.semaphore_signal(barrier, inc=1, device_id=dev(q // 4, lax.rem(q // 2, 2), y, z, lax.rem(q, 2)), device_id_type=MESH)
    for k in range(1, 4):
        for cc in range(2):
            for uu in range(2):
                pl.semaphore_signal(barrier, inc=1, device_id=dev(l, cc, y + k, z, uu), device_id_type=MESH)
                pl.semaphore_signal(barrier, inc=1, device_id=dev(l, cc, y, z + k, uu), device_id_type=MESH)
    pl.semaphore_wait(barrier, 31)

    row = tgt[0:1, :]
    for region in range(G):
        lr, ur = region // 2, region % 2
        slots = lax.broadcasted_iota(jnp.int32, (CAP, row.shape[1]), 0) + region * CAP
        pick = jnp.where(slots == row, 1.0, 0.0).astype(jnp.bfloat16)
        for d in range(3):
            snd[region, :, d * CAP : (d + 1) * CAP] = lax.dot_general(
                cent[d], pick, NT, preferred_element_type=jnp.float32
            ).astype(jnp.bfloat16)
        mine = jnp.logical_and(own, jnp.logical_and(l == lr, u == ur))

        @pl.when(mine)
        def _():
            pltpu.make_async_copy(snd.at[region], panels.at[0, r], relay_rs.at[r]).start()

        @pl.when(jnp.logical_not(mine))
        def _():
            copy(snd.at[region], panels.at[0, r], relay_ss.at[region], relay_rs.at[r], dev(lr, u, y, z, ur)).start()

    sibling = dev(l, 1 - c, y, z, u)
    yp, ym = dev(l, c, y + 1, z, u), dev(l, c, y + 3, z, u)
    zp, zm = dev(l, c, y, z + 1, u), dev(l, c, y, z + 3, u)

    def piece(slot, g):
        return scales.at[slot] if isinstance(g, int) and g == G else panels.at[slot, g]

    def send(kind, src, dst, g, to):
        return copy(piece(src, g), piece(dst, g), ring_ss.at[kind, g], ring_rs.at[kind, g], to)

    def share(slot, g):
        return copy(piece(2 * slot, g), piece(2 * slot + 1, g), sib_ss.at[slot, g], sib_rs.at[slot, g], sibling)

    def send_own(g):
        send(0, 0, 6, g, yp).start()
        send(1, 0, 2, g, ym).start()
        send(2, 0, 10, g, zp).start()
        send(3, 0, 8, g, zm).start()
        share(0, g).start()

    first = 2 * jnp.where(own, l, 1 - l)
    turn = [lax.rem(first + i, G) for i in range(G)]
    for g in turn:
        copy(snd.at[0], panels.at[0, g], relay_ss.at[0], relay_rs.at[g], sibling).wait_recv()
        send_own(g)
    square = jnp.zeros((B, 1), jnp.float32)
    for g in range(G):
        x = panels[0, g].astype(jnp.float32)
        square += jnp.sum(x * x, axis=1, keepdims=True)
    norm = jnp.broadcast_to(jnp.sqrt(square) * (1.0 + 2.0**-7), (B, 128)).T
    scales[0] = norm[0:16, :].astype(jnp.bfloat16)
    send_own(G)

    def block(bi, ai, rows=B, at=0):
        total = None
        for g in range(G):
            part = lax.dot_general(
                panels[bi, g, at : at + rows, :], panels[ai, g], NT, preferred_element_type=jnp.float32
            )
            total = part if total is None else total + part
        inv_a, inv_b = inverse(ai), inverse(bi)
        column = jnp.broadcast_to(inv_b, (128, B)).T[at : at + rows]
        wide = jnp.concatenate([column, column], axis=1)
        scaled = total * wide * (inv_a * 32767.0)
        return (scaled + 12582912.0 - 12582912.0).astype(jnp.int32).astype(jnp.int16)

    def inverse(slot):
        row = scales[slot].astype(jnp.float32)[0:1, :]
        return jnp.where(row > 0.0, 1.0 / row, 0.0)

    def number(yb, zb, hb):
        return 8 * lax.rem(yb, 4) + 2 * lax.rem(zb, 4) + hb

    sent = []

    def deliver(t, bi, ai, b, owner, maybe_self=False, half=None):
        if half is None:
            res[t] = block(bi, ai)
            src, dst, sem = res.at[t], out.at[b], res_rs.at[b]
        else:
            part = pl.ds(half * 128, 128)
            res[t, part, :] = block(bi, ai, 128, half * 128)
            src, dst = res.at[t, part], out.at[b, part]
            sem = res_rs.at[b] if half == 0 else res_rs.at[32 + lax.rem(b, 2)]
        moves = [(src, dst, res_ss.at[t], sem)]
        if half != 1:
            moves.append((scales.at[bi], out_scale.at[b], scale_ss.at[t], scale_rs.at[b]))
        for src, dst, ss, rs in moves:
            remote = copy(src, dst, ss, rs, owner)
            if maybe_self:

                @pl.when(own)
                def _():
                    pltpu.make_async_copy(src, dst, rs).start()

                @pl.when(jnp.logical_not(own))
                def _():
                    remote.start()
            else:
                remote.start()
            sent.append((remote, maybe_self))

    def cols(dz):
        return 0 if dz == 0 else 7 + dz

    def head(j):
        return c if j == 0 else 1 - c

    def home_rows(t, dz):
        for j in range(2):
            deliver(t + j, cols(dz), j, number(y, z + dz, c), dev(l, u, y, z, head(j)), maybe_self=j == 0)

    def home_cols(t, dy):
        for j in range(2):
            deliver(t + j, 2 * dy + j, 0, number(y + dy, z, head(j)), dev(l, u, y, z, c), maybe_self=True)

    def by_y(t, dy, dz, half=None):
        for j in range(2):
            deliver(t + j, cols(dz), 2 * dy + j, number(y, z + dz, c), dev(l, u, y + dy, z, head(j)), half=half)

    def by_z(t, dy, dz, half=None):
        for j in range(2):
            deliver(t + j, 2 * dy + j, cols(dz), number(y + dy, z, head(j)), dev(l, u, y, z + dz, c), half=half)

    def got_share(slot):
        for g in range(G + 1):
            share(slot, g).wait_recv()

    def forward(kind, src, dst, g, to):
        return copy(piece(src, g), piece(dst, g), ring_ss.at[kind, g], ring_rs.at[kind, g], to)

    got_share(0)
    home_rows(0, 0)
    for i, g in enumerate(turn + [G]):
        up = i % 2 == 0
        send(0, 0, 6, g, yp).wait_recv()
        if up:
            forward(4, 6, 4, g, yp).start()
        share(3, g).start()
        send(2, 0, 10, g, zp).wait_recv()
        if up:
            forward(5, 10, 9, g, zp).start()
        send(1, 0, 2, g, ym).wait_recv()
        if not up:
            forward(4, 2, 4, g, ym).start()
        share(1, g).start()
        send(3, 0, 8, g, zm).wait_recv()
        if not up:
            forward(5, 8, 9, g, zm).start()
    got_share(1)
    got_share(3)
    home_rows(2, 1)
    home_rows(4, 3)
    home_cols(6, 1)
    home_cols(8, 3)
    by_y(10, 3, 1)
    by_y(12, 1, 3)
    by_z(14, 1, 1)
    by_z(16, 3, 3)
    for g in turn + [G]:
        forward(4, 6, 4, g, yp).wait_recv()
        share(2, g).start()
    for g in turn + [G]:
        forward(5, 10, 9, g, zp).wait_recv()
    home_rows(18, 2)
    by_y(20, 1, 2)
    by_y(22, 3, 2)
    got_share(2)
    home_cols(24, 2)
    by_z(26, 2, 1)
    by_z(28, 2, 3)
    by_y(30, 2, 2, 0)
    by_z(32, 2, 2, 1)

    for region in range(G):
        mine = jnp.logical_and(own, jnp.logical_and(l == region // 2, u == region % 2))

        @pl.when(jnp.logical_not(mine))
        def _():
            copy(snd.at[region], panels.at[0, r], relay_ss.at[region], relay_rs.at[r], sibling).wait_send()

    for g in range(G + 1):
        for kind in range(6):
            send(kind, 0, 2, g, yp).wait_send()
        for slot in range(4):
            share(slot, g).wait_send()
    for remote, maybe_self in sent:
        if maybe_self:

            @pl.when(jnp.logical_not(own))
            def _():
                remote.wait_send()
        else:
            remote.wait_send()
    for ey in range(4):
        for ez in range(4):
            for h in range(2):
                b = number(y + ey, z + ez, h)
                copy(scales.at[0], out_scale.at[b], scale_ss.at[0], scale_rs.at[b], sibling).wait_recv()
                if (ey, ez) == (2, 2):
                    for half, sem in ((0, res_rs.at[b]), (1, res_rs.at[32 + h])):
                        part = pl.ds(half * 128, 128)
                        copy(res.at[0, part], out.at[b, part], res_ss.at[0], sem, sibling).wait_recv()
                else:
                    copy(res.at[0], out.at[b], res_ss.at[0], res_rs.at[b], sibling).wait_recv()


def gram(cent, tgt):
    dma = pltpu.SemaphoreType.DMA
    return pl.pallas_call(
        gram_kernel,
        out_shape=(
            jax.ShapeDtypeStruct((32, B, B), jnp.int16),
            jax.ShapeDtypeStruct((32, 16, B), jnp.bfloat16),
        ),
        in_specs=[pl.BlockSpec(memory_space=pltpu.VMEM)] * 2,
        out_specs=[pl.BlockSpec(memory_space=pl.ANY)] * 2,
        scratch_shapes=[
            pltpu.VMEM((G, B, F), jnp.bfloat16),
            pltpu.VMEM((11, G, B, F), jnp.bfloat16),
            pltpu.VMEM((11, 16, B), jnp.bfloat16),
            pltpu.VMEM((34, B, B), jnp.int16),
            dma((G,)),
            dma((G,)),
            dma((6, G + 1)),
            dma((6, G + 1)),
            dma((4, G + 1)),
            dma((4, G + 1)),
            dma((34,)),
            dma((34,)),
            dma((34,)),
            dma((32,)),
        ],
        compiler_params=pltpu.CompilerParams(
            collective_id=0, has_side_effects=True, vmem_limit_bytes=50 * 2**20
        ),
        cost_estimate=pl.CostEstimate(flops=13 * 10**9, bytes_accessed=10 * 2**20, transcendentals=0),
        name="gram",
    )(cent, tgt)


W = 1024
T = 128
U = 16


def order_kernel(order, me, q, scale, out, table, even, odd):
    step = pl.program_id(0)

    @pl.when(step == 0)
    def _():
        row = scale[me[0]].astype(jnp.float32)[0:1, :] * (1.0 / (32767.0 * 3.0 * 2048.0))

        def decode(b, _):
            column = jnp.broadcast_to(scale[b].astype(jnp.float32)[0:1, :], (128, B)).T
            for i in range(2):
                lanes = slice(128 * i, 128 * (i + 1))
                values = q[b, :, lanes].astype(jnp.int32).astype(jnp.float32)
                table[pl.ds(b * 2 * B + i, B, stride=2), :] = values * column * row[:, lanes]
            return 0

        lax.fori_loop(0, q.shape[0], decode, 0)

    def gather(rows, t):
        for k in range(0, T, U):
            at = step * W + t * T + k
            loaded = [table[pl.ds(pl.multiple_of(2 * order[at + i], 2), 2), :] for i in range(U)]
            for i in range(U):
                rows[pl.ds(2 * (k + i), 2), :] = loaded[i]

    def flip(rows, t):
        for i in range(2):
            out[0, 128 * i : 128 * (i + 1), t * T : (t + 1) * T] = rows[pl.ds(i, T, stride=2), :].T

    both = (even, odd)
    gather(even, 0)
    for t in range(1, W // T):
        flip(both[(t - 1) % 2], t - 1)
        gather(both[t % 2], t)
    flip(both[(W // T - 1) % 2], W // T - 1)


def ordered(order, me, q, scale):
    n = order.shape[0]
    return pl.pallas_call(
        order_kernel,
        out_shape=jax.ShapeDtypeStruct((1, B, n), jnp.float32),
        grid_spec=pltpu.PrefetchScalarGridSpec(
            num_scalar_prefetch=2,
            grid=(n // W,),
            in_specs=[
                pl.BlockSpec(q.shape, lambda i, o, m: (0, 0, 0), pipeline_mode=pl.Buffered(1)),
                pl.BlockSpec(scale.shape, lambda i, o, m: (0, 0, 0), pipeline_mode=pl.Buffered(1)),
            ],
            out_specs=pl.BlockSpec((1, B, W), lambda i, o, m: (0, 0, i)),
            scratch_shapes=[
                pltpu.VMEM((2 * n, 128), jnp.float32),
                pltpu.VMEM((2 * T, 128), jnp.float32),
                pltpu.VMEM((2 * T, 128), jnp.float32),
            ],
        ),
        compiler_params=pltpu.CompilerParams(vmem_limit_bytes=40 * 2**20),
        cost_estimate=pl.CostEstimate(flops=0, bytes_accessed=6 * n * B, transcendentals=0),
        name="ordered",
    )(order, me, q, scale)


def local(coords, transform, labels, subject_order):
    verts = coords.shape[2] * lax.axis_size("region")
    moved = jnp.stack(
        [
            transform[:, d, 0:1] * coords[:, 0, :]
            + transform[:, d, 1:2] * coords[:, 1, :]
            + transform[:, d, 2:3] * coords[:, 2, :]
            for d in range(3)
        ]
    )
    totals = lax.psum(jnp.sum(moved, axis=2), "region")
    cent = (moved - (totals / verts)[:, :, None]).astype(jnp.bfloat16)
    lab = labels[:, 0]
    n = lab.shape[0]
    before = jnp.arange(n)[:, None] < jnp.arange(n)[None, :]
    rank = jnp.sum(jnp.where((labels == lab[None, :]) & before, 1, 0), axis=0)
    tgt = jnp.broadcast_to((lab * CAP + rank)[None, :], (8, n))
    return ordered(subject_order, lax.axis_index("subj")[None], *gram(cent, tgt))


def solution(mesh):
    placed = (P("subj", None, "region"), P("subj", None, None), P("region", None), P())
    return jax.shard_map(
        local, mesh=mesh, in_specs=placed, out_specs=P("region", "subj", None), check_vma=False
    )
```

```python
import functools

import jax
import jax.numpy as jnp
from jax import lax
from jax.experimental import pallas as pl
from jax.experimental.pallas import tpu as pltpu
from jax.sharding import PartitionSpec as P

CAP = 256
B = 256
H = 128
G = 4
F = 3 * CAP
MESH = pl.DeviceIdType.MESH
NT = (((1,), (1,)), ((), ()))


def dev(l, c, y, z, u):
    return (2 * l + c, 8 * lax.rem(y, 4) + 2 * lax.rem(z, 4) + u)


def gram_kernel(cent, tgt, out, out_scale, snd, panels, scales, res, relay_ss, relay_rs, ring_ss, ring_rs, sib_ss, sib_rs, res_ss, res_rs, scale_ss, scale_rs):
    r, s = lax.axis_index("region"), lax.axis_index("subj")
    l, c = r // 2, lax.rem(r, 2)
    y, z, u = s // 8, lax.rem(s // 2, 4), lax.rem(s, 2)
    barrier = pltpu.get_barrier_semaphore()
    own = c == u

    def copy(src, dst, ss, rs, to):
        return pltpu.make_async_remote_copy(
            src_ref=src, dst_ref=dst, send_sem=ss, recv_sem=rs, device_id=to, device_id_type=MESH
        )

    for k in range(1, 8):
        q = lax.rem(l * 4 + c * 2 + u + k, 8)
        pl.semaphore_signal(barrier, inc=1, device_id=dev(q // 4, lax.rem(q // 2, 2), y, z, lax.rem(q, 2)), device_id_type=MESH)
    for k in range(1, 4):
        for cc in range(2):
            for uu in range(2):
                pl.semaphore_signal(barrier, inc=1, device_id=dev(l, cc, y + k, z, uu), device_id_type=MESH)
                pl.semaphore_signal(barrier, inc=1, device_id=dev(l, cc, y, z + k, uu), device_id_type=MESH)
    pl.semaphore_wait(barrier, 31)

    def relay(half, region):
        lr, ur = region // 2, region % 2
        mine = jnp.logical_and(own, jnp.logical_and(l == lr, u == ur))
        src, dst, rs = snd.at[half, region], panels.at[r, 0, half], relay_rs.at[half, r]
        return mine, src, dst, rs, copy(src, dst, relay_ss.at[half, region], rs, dev(lr, u, y, z, ur))

    row = tgt[0:1, :]
    slots = lax.broadcasted_iota(jnp.int32, (CAP, row.shape[1]), 0)
    for half in range(2):
        for region in range(G):
            pick = jnp.where(slots + region * CAP == row, 1.0, 0.0).astype(jnp.bfloat16)
            for d in range(3):
                snd[half, region, :, d * CAP : (d + 1) * CAP] = lax.dot_general(
                    cent[d, half * H : (half + 1) * H, :], pick, NT, preferred_element_type=jnp.float32
                ).astype(jnp.bfloat16)
            mine, src, dst, rs, remote = relay(half, region)

            @pl.when(mine)
            def _():
                pltpu.make_async_copy(src, dst, rs).start()

            @pl.when(jnp.logical_not(mine))
            def _():
                remote.start()

    sibling = dev(l, 1 - c, y, z, u)
    yp, ym = dev(l, c, y + 1, z, u), dev(l, c, y + 3, z, u)
    zp, zm = dev(l, c, y, z + 1, u), dev(l, c, y, z + 3, u)

    def piece(slot, half, g):
        return scales.at[half, slot] if isinstance(g, int) and g == G else panels.at[g, slot, half]

    def place(slot):
        dy, dz = {2: 1, 4: 3, 6: 2}.get(slot // 2 * 2, 0), {8: 1, 9: 3, 10: 2}.get(slot, 0)
        return (y + (dy if slot < 8 else 0), z + dz, c if slot >= 8 or slot % 2 == 0 else 1 - c)

    def send(kind, src, dst, half, g, to):
        at = (kind, half, g)
        return copy(piece(src, half, g), piece(dst, half, g), ring_ss.at[at], ring_rs.at[at], to)

    def share(pos, half, g):
        at = (pos, half, g)
        return copy(piece(2 * pos, half, g), piece(2 * pos + 1, half, g), sib_ss.at[at], sib_rs.at[at], sibling)

    def send_own(half, g):
        send(0, 0, 4, half, g, yp).start()
        send(1, 0, 2, half, g, ym).start()
        send(2, 0, 9, half, g, zp).start()
        send(3, 0, 8, half, g, zm).start()
        share(0, half, g).start()

    first = 2 * jnp.where(own, l, 1 - l)
    turn = [lax.rem(first + i, G) for i in range(G)]
    for half in range(2):
        for g in turn:
            copy(snd.at[0, 0], panels.at[g, 0, half], relay_ss.at[0, 0], relay_rs.at[half, g], sibling).wait_recv()
            send_own(half, g)
        square = jnp.zeros((H, 1), jnp.float32)
        for g in range(G):
            x = panels[g, 0, half].astype(jnp.float32)
            square += jnp.sum(x * x, axis=1, keepdims=True)
        norm = jnp.broadcast_to(jnp.sqrt(square) * (1.0 + 2.0**-7), (H, 128)).T
        scales[half, 0] = norm[0:16, :].astype(jnp.bfloat16)
        send_own(half, G)

    def inverse(half, slot):
        row = scales[half, slot].astype(jnp.float32)[0:1, :]
        return jnp.where(row > 0.0, 1.0 / row, 0.0)

    def products(bs, b_halves, as_, a_halves):
        def rows(g, slots, halves):
            some = slice(halves[0], halves[-1] + 1)
            return panels[g, slots, some].reshape(-1, F)

        def inverses(slots, halves):
            return [inverse(half, k) for k in range(slots.start, slots.stop) for half in halves]

        total = None
        for g in range(G):
            part = lax.dot_general(rows(g, bs, b_halves), rows(g, as_, a_halves), NT, preferred_element_type=jnp.float32)
            total = part if total is None else total + part
        across, down = inverses(as_, a_halves), inverses(bs, b_halves)
        down = [jnp.broadcast_to(v, (128, H)).T for v in down]
        return [
            [
                total[i * H : (i + 1) * H, k * H : (k + 1) * H] * down[i] * (across[k] * 32767.0) + 12582912.0 - 12582912.0
                for k in range(len(across))
            ]
            for i in range(len(down))
        ]

    blocks = {}

    def deliver(b, hb, a, a_halves, tiles):
        number = 8 * lax.rem(place(b)[0], 4) + 2 * lax.rem(place(b)[1], 4) + place(b)[2]
        owner = dev(l, u, *place(a))
        t, b_halves = blocks.setdefault((b, a), (len(blocks), set()))
        b_halves.add(hb)
        at = (pl.ds(hb * H, H), pl.ds(a_halves[0] * H, len(a_halves) * H))
        for ha, tile in zip(a_halves, tiles, strict=True):
            res[t, hb * H : (hb + 1) * H, ha * H : (ha + 1) * H] = tile.astype(jnp.int32).astype(jnp.int16)
        moves = [(res.at[(t, *at)], out.at[(number, *at)], res_ss.at[t], res_rs.at[number])]
        if 0 in a_halves:
            moves.append((scales.at[hb, b], out_scale.at[number, hb], scale_ss.at[t], scale_rs.at[number]))
        for src, dst, ss, rs in moves:
            remote = copy(src, dst, ss, rs, owner)
            if a == 0:

                @pl.when(own)
                def _():
                    pltpu.make_async_copy(src, dst, rs).start()

                @pl.when(jnp.logical_not(own))
                def _():
                    remote.start()
            else:
                remote.start()

    BOTH = (0, 1)

    def straight(bs, b_halves, as_, a_halves, keep=lambda b, a: True):
        out_of = products(bs, b_halves, as_, a_halves)
        n, m = len(b_halves), len(a_halves)
        for i, b in enumerate(range(bs.start, bs.stop)):
            for p, hb in enumerate(b_halves):
                for k, a in enumerate(range(as_.start, as_.stop)):
                    if keep(b, a):
                        deliver(b, hb, a, a_halves, out_of[i * n + p][k * m : (k + 1) * m])
        return out_of

    def turned(out_of, bs, b_halves, as_, a_halves, keep=lambda b, a: True):
        n, m = len(b_halves), len(a_halves)
        for k, a in enumerate(range(as_.start, as_.stop)):
            for q, ha in enumerate(a_halves):
                for i, b in enumerate(range(bs.start, bs.stop)):
                    if keep(b, a):
                        deliver(a, ha, b, b_halves, [out_of[i * n + p][k * m + q].T for p in range(n)])

    def got_share(pos, half):
        for g in range(G + 1):
            share(pos, half, g).wait_recv()

    for half in range(2):
        got_share(0, half)
    straight(slice(0, 1), BOTH, slice(0, 2), BOTH)
    for half in range(2):
        for i, g in enumerate(turn + [G]):
            up = i % 2 == 0
            send(0, 0, 4, half, g, yp).wait_recv()
            if up:
                send(4, 4, 6, half, g, yp).start()
            share(2, half, g).start()
            send(2, 0, 9, half, g, zp).wait_recv()
            if up:
                send(5, 9, 10, half, g, zp).start()
            send(1, 0, 2, half, g, ym).wait_recv()
            if not up:
                send(4, 2, 6, half, g, ym).start()
            share(1, half, g).start()
            send(3, 0, 8, half, g, zm).wait_recv()
            if not up:
                send(5, 8, 10, half, g, zm).start()
        straight(slice(8, 10), (half,), slice(0, 2), BOTH)
        got_share(1, half)
        got_share(2, half)
        straight(slice(2, 6), (half,), slice(0, 1), BOTH)
        for hb, has in (((0,), (0,)),) if half == 0 else (((1,), BOTH), ((0,), (1,))):
            cross = slice(8, 10), hb, slice(4, 6), has
            turned(straight(*cross), *cross)
    for half in range(2):
        here = (half,)
        for g in turn + [G]:
            send(4, 4, 6, half, g, yp).wait_recv()
            share(3, half, g).start()
        for g in turn + [G]:
            send(5, 9, 10, half, g, zp).wait_recv()
        far = slice(0, 6), BOTH, slice(10, 11), here
        turned(products(*far), *far)
        got_share(3, half)
        straight(slice(6, 8), here, slice(0, 1), BOTH)
        straight(slice(6, 8), here, slice(8, 10), BOTH)
        if half == 0:
            straight(slice(10, 11), (0,), slice(6, 8), (0,))
        else:
            opposite = slice(6, 8), (1,), slice(10, 11), BOTH
            tiles = straight(*opposite)
            turned([row[:1] for row in tiles], slice(6, 8), (1,), slice(10, 11), (0,))

    for half in range(2):
        for region in range(G):
            mine, *_, remote = relay(half, region)

            @pl.when(jnp.logical_not(mine))
            def _():
                remote.wait_send()

        for g in range(G + 1):
            for kind in range(6):
                send(kind, 0, 2, half, g, yp).wait_send()
            for pos in range(4):
                share(pos, half, g).wait_send()
    for (_, a), (t, halves) in blocks.items():
        part = pl.ds(min(halves) * H, len(halves) * H)
        some = pl.ds(min(halves), len(halves))

        def left(t=t, part=part, some=some):
            copy(res.at[t, part], out.at[0, part], res_ss.at[t], res_rs.at[0], sibling).wait_send()
            copy(out_scale.at[0, some], out_scale.at[0, some], scale_ss.at[t], scale_rs.at[0], sibling).wait_send()

        if a == 0:
            pl.when(jnp.logical_not(own))(left)
        else:
            left()
    for b in range(32):
        copy(res.at[0], out.at[b], res_ss.at[0], res_rs.at[b], sibling).wait_recv()
        copy(out_scale.at[b], out_scale.at[b], scale_ss.at[0], scale_rs.at[b], sibling).wait_recv()


def gram(cent, tgt):
    dma = pltpu.SemaphoreType.DMA
    return pl.pallas_call(
        gram_kernel,
        out_shape=(
            jax.ShapeDtypeStruct((32, B, B), jnp.int16),
            jax.ShapeDtypeStruct((32, 2, 16, H), jnp.bfloat16),
        ),
        in_specs=[pl.BlockSpec(memory_space=pltpu.VMEM)] * 2,
        out_specs=[pl.BlockSpec(memory_space=pl.ANY)] * 2,
        scratch_shapes=[
            pltpu.VMEM((2, G, H, F), jnp.bfloat16),
            pltpu.VMEM((G, 11, 2, H, F), jnp.bfloat16),
            pltpu.VMEM((2, 11, 16, H), jnp.bfloat16),
            pltpu.VMEM((34, B, B), jnp.int16),
            dma((2, G)),
            dma((2, G)),
            dma((6, 2, G + 1)),
            dma((6, 2, G + 1)),
            dma((4, 2, G + 1)),
            dma((4, 2, G + 1)),
            dma((34,)),
            dma((32,)),
            dma((34,)),
            dma((32,)),
        ],
        compiler_params=pltpu.CompilerParams(
            collective_id=0, has_side_effects=True, vmem_limit_bytes=50 * 2**20
        ),
        cost_estimate=pl.CostEstimate(flops=13 * 10**9, bytes_accessed=10 * 2**20, transcendentals=0),
        name="gram",
    )(cent, tgt)


W = 1024
T = 128
U = 16


def order_kernel(order, me, q, scale, out, table, even, odd):
    step = pl.program_id(0)

    @pl.when(step == 0)
    def _():
        def scale_row(b):
            halves = [scale[b, half].astype(jnp.float32)[0:1, :] for half in range(2)]
            return jnp.concatenate(halves, axis=1)

        row = scale_row(me[0]) * (1.0 / (32767.0 * 3.0 * 2048.0))

        def decode(b, _):
            column = jnp.broadcast_to(scale_row(b), (128, B)).T
            for i in range(2):
                lanes = slice(128 * i, 128 * (i + 1))
                values = q[b, :, lanes].astype(jnp.int32).astype(jnp.float32)
                table[pl.ds(b * 2 * B + i, B, stride=2), :] = values * column * row[:, lanes]
            return 0

        lax.fori_loop(0, q.shape[0], decode, 0)

    def gather(rows, t):
        for k in range(0, T, U):
            at = step * W + t * T + k
            loaded = [table[pl.ds(pl.multiple_of(2 * order[at + i], 2), 2), :] for i in range(U)]
            for i in range(U):
                rows[pl.ds(2 * (k + i), 2), :] = loaded[i]

    def flip(rows, t):
        for i in range(2):
            out[0, 128 * i : 128 * (i + 1), t * T : (t + 1) * T] = rows[pl.ds(i, T, stride=2), :].T

    both = (even, odd)
    gather(even, 0)
    for t in range(1, W // T):
        flip(both[(t - 1) % 2], t - 1)
        gather(both[t % 2], t)
    flip(both[(W // T - 1) % 2], W // T - 1)


def ordered(order, me, q, scale):
    n = order.shape[0]
    return pl.pallas_call(
        order_kernel,
        out_shape=jax.ShapeDtypeStruct((1, B, n), jnp.float32),
        grid_spec=pltpu.PrefetchScalarGridSpec(
            num_scalar_prefetch=2,
            grid=(n // W,),
            in_specs=[
                pl.BlockSpec(q.shape, lambda i, o, m: (0, 0, 0), pipeline_mode=pl.Buffered(1)),
                pl.BlockSpec(scale.shape, lambda i, o, m: (0, 0, 0, 0), pipeline_mode=pl.Buffered(1)),
            ],
            out_specs=pl.BlockSpec((1, B, W), lambda i, o, m: (0, 0, i)),
            scratch_shapes=[
                pltpu.VMEM((2 * n, 128), jnp.float32),
                pltpu.VMEM((2 * T, 128), jnp.float32),
                pltpu.VMEM((2 * T, 128), jnp.float32),
            ],
        ),
        compiler_params=pltpu.CompilerParams(vmem_limit_bytes=40 * 2**20),
        cost_estimate=pl.CostEstimate(flops=0, bytes_accessed=6 * n * B, transcendentals=0),
        name="ordered",
    )(order, me, q, scale)


def local(coords, transform, labels, subject_order):
    verts = coords.shape[2] * lax.axis_size("region")
    moved = jnp.stack(
        [
            transform[:, d, 0:1] * coords[:, 0, :]
            + transform[:, d, 1:2] * coords[:, 1, :]
            + transform[:, d, 2:3] * coords[:, 2, :]
            for d in range(3)
        ]
    )
    totals = lax.psum(jnp.sum(moved, axis=2), "region")
    cent = (moved - (totals / verts)[:, :, None]).astype(jnp.bfloat16)
    lab = labels[:, 0]
    n = lab.shape[0]
    before = jnp.arange(n)[:, None] < jnp.arange(n)[None, :]
    rank = jnp.sum(jnp.where((labels == lab[None, :]) & before, 1, 0), axis=0)
    tgt = jnp.broadcast_to((lab * CAP + rank)[None, :], (8, n))
    return ordered(subject_order, lax.axis_index("subj")[None], *gram(cent, tgt))


def solution(mesh):
    placed = (P("subj", None, "region"), P("subj", None, None), P("region", None), P())
    return jax.shard_map(
        local, mesh=mesh, in_specs=placed, out_specs=P("region", "subj", None), check_vma=False
    )
```

```python
import functools

import jax
import jax.numpy as jnp
from jax import lax
from jax.experimental import pallas as pl
from jax.experimental.pallas import tpu as pltpu
from jax.sharding import PartitionSpec as P

CAP = 256
B = 256
H = 128
G = 4
F = 3 * CAP
MESH = pl.DeviceIdType.MESH
NT = (((1,), (1,)), ((), ()))


def dev(l, c, y, z, u):
    return (2 * l + c, 8 * lax.rem(y, 4) + 2 * lax.rem(z, 4) + u)


def gram_kernel(moved, part, labels, out, out_scale, cent, parts, snd, panels, scales, res, sum_ss, sum_rs, relay_ss, relay_rs, ring_ss, ring_rs, sib_ss, sib_rs, res_ss, res_rs, scale_ss, scale_rs):
    r, s = lax.axis_index("region"), lax.axis_index("subj")
    l, c = r // 2, lax.rem(r, 2)
    y, z, u = s // 8, lax.rem(s // 2, 4), lax.rem(s, 2)
    barrier = pltpu.get_barrier_semaphore()
    own = c == u

    def copy(src, dst, ss, rs, to):
        return pltpu.make_async_remote_copy(
            src_ref=src, dst_ref=dst, send_sem=ss, recv_sem=rs, device_id=to, device_id_type=MESH
        )

    for k in range(1, 8):
        q = lax.rem(l * 4 + c * 2 + u + k, 8)
        pl.semaphore_signal(barrier, inc=1, device_id=dev(q // 4, lax.rem(q // 2, 2), y, z, lax.rem(q, 2)), device_id_type=MESH)
    for k in range(1, 4):
        for cc in range(2):
            for uu in range(2):
                pl.semaphore_signal(barrier, inc=1, device_id=dev(l, cc, y + k, z, uu), device_id_type=MESH)
                pl.semaphore_signal(barrier, inc=1, device_id=dev(l, cc, y, z + k, uu), device_id_type=MESH)
    lab = labels[...].astype(jnp.float32)[0:1, :]
    n = lab.shape[1]
    same = jnp.broadcast_to(lab, (128, n)).T[:, 0:1] == lab
    before = lax.broadcasted_iota(jnp.int32, (n, n), 0) < lax.broadcasted_iota(jnp.int32, (n, n), 1)
    rank = jnp.sum(jnp.where(jnp.logical_and(same, before), 1.0, 0.0), axis=0, keepdims=True)
    row = (lab * CAP + rank).astype(jnp.int32)
    pl.semaphore_wait(barrier, 31)

    def sums(k, owner):
        return copy(part, parts.at[owner], sum_ss.at[k - 1], sum_rs.at[owner], (lax.rem(r + k, G), s))

    for k in range(1, G):
        sums(k, r).start()
    parts[r] = part[...]
    for k in range(1, G):
        sums(k, lax.rem(r + k, G)).wait_recv()
    mean = (parts[0] + parts[1] + parts[2] + parts[3]) * (1.0 / (G * moved.shape[2]))
    for d in range(3):
        column = jnp.broadcast_to(mean[d : d + 1], (128, B)).T
        cent[d] = (moved[d] - jnp.concatenate([column] * (moved.shape[2] // 128), axis=1)).astype(jnp.bfloat16)

    def relay(half, region):
        lr, ur = region // 2, region % 2
        mine = jnp.logical_and(own, jnp.logical_and(l == lr, u == ur))
        src, dst, rs = snd.at[half, region], panels.at[r, 0, half], relay_rs.at[half, r]
        return mine, src, dst, rs, copy(src, dst, relay_ss.at[half, region], rs, dev(lr, u, y, z, ur))

    slots = lax.broadcasted_iota(jnp.int32, (CAP, row.shape[1]), 0)
    for half in range(2):
        for region in range(G):
            pick = jnp.where(slots + region * CAP == row, 1.0, 0.0).astype(jnp.bfloat16)
            found = lax.dot_general(
                cent[:, half * H : (half + 1) * H, :].reshape(3 * H, -1), pick, NT, preferred_element_type=jnp.float32
            ).astype(jnp.bfloat16)
            for d in range(3):
                snd[half, region, :, d * CAP : (d + 1) * CAP] = found[d * H : (d + 1) * H]
            mine, src, dst, rs, remote = relay(half, region)

            @pl.when(mine)
            def _():
                pltpu.make_async_copy(src, dst, rs).start()

            @pl.when(jnp.logical_not(mine))
            def _():
                remote.start()

    sibling = dev(l, 1 - c, y, z, u)
    yp, ym = dev(l, c, y + 1, z, u), dev(l, c, y + 3, z, u)
    zp, zm = dev(l, c, y, z + 1, u), dev(l, c, y, z + 3, u)

    def piece(slot, half, g):
        return scales.at[half, slot] if isinstance(g, int) and g == G else panels.at[g, slot, half]

    def place(slot):
        dy, dz = {2: 1, 4: 3, 6: 2}.get(slot // 2 * 2, 0), {8: 1, 9: 3, 10: 2}.get(slot, 0)
        return (y + (dy if slot < 8 else 0), z + dz, c if slot >= 8 or slot % 2 == 0 else 1 - c)

    def send(kind, src, dst, half, g, to):
        at = (kind, half, g)
        return copy(piece(src, half, g), piece(dst, half, g), ring_ss.at[at], ring_rs.at[at], to)

    def share(pos, half, g):
        at = (pos, half, g)
        return copy(piece(2 * pos, half, g), piece(2 * pos + 1, half, g), sib_ss.at[at], sib_rs.at[at], sibling)

    def send_own(half, g):
        send(0, 0, 4, half, g, yp).start()
        send(1, 0, 2, half, g, ym).start()
        send(2, 0, 9, half, g, zp).start()
        send(3, 0, 8, half, g, zm).start()
        share(0, half, g).start()

    first = 2 * jnp.where(own, l, 1 - l)
    turn = [lax.rem(first + i, G) for i in range(G)]
    for half in range(2):
        for g in turn:
            copy(snd.at[0, 0], panels.at[g, 0, half], relay_ss.at[0, 0], relay_rs.at[half, g], sibling).wait_recv()
            send_own(half, g)
        square = jnp.zeros((H, 1), jnp.float32)
        for g in range(G):
            x = panels[g, 0, half].astype(jnp.float32)
            square += jnp.sum(x * x, axis=1, keepdims=True)
        norm = jnp.broadcast_to(jnp.sqrt(square) * (1.0 + 2.0**-7), (H, 128)).T
        scales[half, 0] = norm[0:16, :].astype(jnp.bfloat16)
        send_own(half, G)

    def inverse(half, slot):
        row = scales[half, slot].astype(jnp.float32)[0:1, :]
        return jnp.where(row > 0.0, 1.0 / row, 0.0)

    def products(bs, b_halves, as_, a_halves):
        def rows(g, slots, halves):
            some = slice(halves[0], halves[-1] + 1)
            return panels[g, slots, some].reshape(-1, F)

        def inverses(slots, halves):
            return [inverse(half, k) for k in range(slots.start, slots.stop) for half in halves]

        total = None
        for g in range(G):
            part = lax.dot_general(rows(g, bs, b_halves), rows(g, as_, a_halves), NT, preferred_element_type=jnp.float32)
            total = part if total is None else total + part
        across, down = inverses(as_, a_halves), inverses(bs, b_halves)
        down = [jnp.broadcast_to(v, (128, H)).T for v in down]
        return [
            [
                total[i * H : (i + 1) * H, k * H : (k + 1) * H] * down[i] * (across[k] * 32767.0) + 12582912.0 - 12582912.0
                for k in range(len(across))
            ]
            for i in range(len(down))
        ]

    blocks = {}
    late = []

    def deliver(b, hb, a, a_halves, tiles):
        number = 8 * lax.rem(place(b)[0], 4) + 2 * lax.rem(place(b)[1], 4) + place(b)[2]
        owner = dev(l, u, *place(a))
        t, b_halves = blocks.setdefault((b, a), (len(blocks), set()))
        b_halves.add(hb)
        at = (pl.ds(hb * H, H), pl.ds(a_halves[0] * H, len(a_halves) * H))
        for ha, tile in zip(a_halves, tiles, strict=True):
            res[t, hb * H : (hb + 1) * H, ha * H : (ha + 1) * H] = tile.astype(jnp.int32).astype(jnp.int16)
        moves = [(res.at[(t, *at)], out.at[(number, *at)], res_ss.at[t], res_rs.at[number])]
        if 0 in a_halves:
            moves.append((scales.at[hb, b], out_scale.at[number, hb], scale_ss.at[t], scale_rs.at[number]))
        for src, dst, ss, rs in moves:
            remote = copy(src, dst, ss, rs, owner)
            if a == 0:

                @pl.when(own)
                def _():
                    pltpu.make_async_copy(src, dst, rs).start()

                @pl.when(jnp.logical_not(own))
                def _():
                    remote.start()
            elif a == 1 or late is None:
                remote.start()
            else:
                across = place(a)[2] != u
                pl.when(across)(remote.start)
                late.append((jnp.logical_not(across), remote))

    def release():
        for there, remote in late:
            pl.when(there)(remote.start)

    BOTH = (0, 1)

    def straight(bs, b_halves, as_, a_halves, keep=lambda b, a: True):
        out_of = products(bs, b_halves, as_, a_halves)
        n, m = len(b_halves), len(a_halves)
        for i, b in enumerate(range(bs.start, bs.stop)):
            for p, hb in enumerate(b_halves):
                for k, a in enumerate(range(as_.start, as_.stop)):
                    if keep(b, a):
                        deliver(b, hb, a, a_halves, out_of[i * n + p][k * m : (k + 1) * m])
        return out_of

    def turned(out_of, bs, b_halves, as_, a_halves, keep=lambda b, a: True):
        n, m = len(b_halves), len(a_halves)
        for k, a in enumerate(range(as_.start, as_.stop)):
            for q, ha in enumerate(a_halves):
                for i, b in enumerate(range(bs.start, bs.stop)):
                    if keep(b, a):
                        deliver(a, ha, b, b_halves, [out_of[i * n + p][k * m + q].T for p in range(n)])

    def got_share(pos, half):
        for g in range(G + 1):
            share(pos, half, g).wait_recv()

    for half in range(2):
        got_share(0, half)
    straight(slice(0, 1), BOTH, slice(0, 2), BOTH)
    for half in range(2):
        for i, g in enumerate(turn + [G]):
            up = i % 2 == 0
            send(0, 0, 4, half, g, yp).wait_recv()
            if up:
                send(4, 4, 6, half, g, yp).start()
            share(2, half, g).start()
            send(2, 0, 9, half, g, zp).wait_recv()
            if up:
                send(5, 9, 10, half, g, zp).start()
            send(1, 0, 2, half, g, ym).wait_recv()
            if not up:
                send(4, 2, 6, half, g, ym).start()
            share(1, half, g).start()
            send(3, 0, 8, half, g, zm).wait_recv()
            if not up:
                send(5, 8, 10, half, g, zm).start()
        straight(slice(8, 10), (half,), slice(0, 2), BOTH)
        got_share(1, half)
        got_share(2, half)
        straight(slice(2, 6), (half,), slice(0, 1), BOTH)
        for hb, has in (((0,), (0,)),) if half == 0 else (((1,), BOTH), ((0,), (1,))):
            cross = slice(8, 10), hb, slice(4, 6), has
            turned(straight(*cross), *cross)
    for half in range(2):
        here = (half,)
        for g in turn + [G]:
            send(4, 4, 6, half, g, yp).wait_recv()
            share(3, half, g).start()
        for g in turn + [G]:
            send(5, 9, 10, half, g, zp).wait_recv()
        if half == 1:
            release()
            late = None
        far = slice(0, 6), BOTH, slice(10, 11), here
        turned(products(*far), *far)
        got_share(3, half)
        straight(slice(6, 8), here, slice(0, 1), BOTH)
        straight(slice(6, 8), here, slice(8, 10), BOTH)
        if half == 0:
            straight(slice(10, 11), (0,), slice(6, 8), (0,))
        else:
            opposite = slice(6, 8), (1,), slice(10, 11), BOTH
            tiles = straight(*opposite)
            turned([row[:1] for row in tiles], slice(6, 8), (1,), slice(10, 11), (0,))

    for k in range(1, G):
        sums(k, r).wait_send()
    for half in range(2):
        for region in range(G):
            mine, *_, remote = relay(half, region)

            @pl.when(jnp.logical_not(mine))
            def _():
                remote.wait_send()

        for g in range(G + 1):
            for kind in range(6):
                send(kind, 0, 2, half, g, yp).wait_send()
            for pos in range(4):
                share(pos, half, g).wait_send()
    for (_, a), (t, halves) in blocks.items():
        part = pl.ds(min(halves) * H, len(halves) * H)
        some = pl.ds(min(halves), len(halves))

        def left(t=t, part=part, some=some):
            copy(res.at[t, part], out.at[0, part], res_ss.at[t], res_rs.at[0], sibling).wait_send()
            copy(out_scale.at[0, some], out_scale.at[0, some], scale_ss.at[t], scale_rs.at[0], sibling).wait_send()

        if a == 0:
            pl.when(jnp.logical_not(own))(left)
        else:
            left()
    for b in range(32):
        copy(res.at[0], out.at[b], res_ss.at[0], res_rs.at[b], sibling).wait_recv()
        copy(out_scale.at[b], out_scale.at[b], scale_ss.at[0], scale_rs.at[b], sibling).wait_recv()


def gram(moved, part, labels):
    dma = pltpu.SemaphoreType.DMA
    return pl.pallas_call(
        gram_kernel,
        out_shape=(
            jax.ShapeDtypeStruct((32, B, B), jnp.int16),
            jax.ShapeDtypeStruct((32, 2, 16, H), jnp.bfloat16),
        ),
        in_specs=[pl.BlockSpec(memory_space=pltpu.VMEM)] * 3,
        out_specs=[pl.BlockSpec(memory_space=pl.ANY)] * 2,
        scratch_shapes=[
            pltpu.VMEM(moved.shape, jnp.bfloat16),
            pltpu.VMEM((G, 8, B), jnp.float32),
            pltpu.VMEM((2, G, H, F), jnp.bfloat16),
            pltpu.VMEM((G, 11, 2, H, F), jnp.bfloat16),
            pltpu.VMEM((2, 11, 16, H), jnp.bfloat16),
            pltpu.VMEM((34, B, B), jnp.int16),
            dma((G - 1,)),
            dma((G,)),
            dma((2, G)),
            dma((2, G)),
            dma((6, 2, G + 1)),
            dma((6, 2, G + 1)),
            dma((4, 2, G + 1)),
            dma((4, 2, G + 1)),
            dma((34,)),
            dma((32,)),
            dma((34,)),
            dma((32,)),
        ],
        compiler_params=pltpu.CompilerParams(
            collective_id=0, has_side_effects=True, vmem_limit_bytes=50 * 2**20
        ),
        cost_estimate=pl.CostEstimate(flops=13 * 10**9, bytes_accessed=10 * 2**20, transcendentals=0),
        name="gram",
    )(moved, part, labels)


W = 1024
T = 128
U = 16


def order_kernel(order, me, q_hbm, scale, out, q, table, even, odd, sems):
    step = pl.program_id(0)

    @pl.when(step == 0)
    def _():
        def scale_row(b):
            halves = [scale[b, half].astype(jnp.float32)[0:1, :] for half in range(2)]
            return jnp.concatenate(halves, axis=1)

        row = scale_row(me[0]) * (1.0 / (32767.0 * 3.0 * 2048.0))

        def decode(b, _):
            column = jnp.broadcast_to(scale_row(b), (128, B)).T
            for i in range(2):
                lanes = slice(128 * i, 128 * (i + 1))
                values = q[b, :, lanes].astype(jnp.int32).astype(jnp.float32)
                table[pl.ds(b * 2 * B + i, B, stride=2), :] = values * column * row[:, lanes]
            return 0

        def fetch(k):
            some = pl.ds(k * 4, 4)
            return pltpu.make_async_copy(q_hbm.at[some], q.at[some], sems.at[k])

        for k in range(8):
            fetch(k).start()
        for k in range(8):
            fetch(k).wait()
            lax.fori_loop(4 * k, 4 * k + 4, decode, 0)

    def gather(rows, t):
        for k in range(0, T, U):
            at = step * W + t * T + k
            loaded = [table[pl.ds(pl.multiple_of(2 * order[at + i], 2), 2), :] for i in range(U)]
            for i in range(U):
                rows[pl.ds(2 * (k + i), 2), :] = loaded[i]

    def flip(rows, t):
        for i in range(2):
            out[0, 128 * i : 128 * (i + 1), t * T : (t + 1) * T] = rows[pl.ds(i, T, stride=2), :].T

    both = (even, odd)
    gather(even, 0)
    for t in range(1, W // T):
        flip(both[(t - 1) % 2], t - 1)
        gather(both[t % 2], t)
    flip(both[(W // T - 1) % 2], W // T - 1)


def ordered(order, me, q, scale):
    n = order.shape[0]
    return pl.pallas_call(
        order_kernel,
        out_shape=jax.ShapeDtypeStruct((1, B, n), jnp.float32),
        grid_spec=pltpu.PrefetchScalarGridSpec(
            num_scalar_prefetch=2,
            grid=(n // W,),
            in_specs=[
                pl.BlockSpec(memory_space=pl.ANY),
                pl.BlockSpec(scale.shape, lambda i, o, m: (0, 0, 0, 0), pipeline_mode=pl.Buffered(1)),
            ],
            out_specs=pl.BlockSpec((1, B, W), lambda i, o, m: (0, 0, i)),
            scratch_shapes=[
                pltpu.VMEM(q.shape, q.dtype),
                pltpu.VMEM((2 * n, 128), jnp.float32),
                pltpu.VMEM((2 * T, 128), jnp.float32),
                pltpu.VMEM((2 * T, 128), jnp.float32),
                pltpu.SemaphoreType.DMA((8,)),
            ],
        ),
        compiler_params=pltpu.CompilerParams(vmem_limit_bytes=58 * 2**20),
        cost_estimate=pl.CostEstimate(flops=0, bytes_accessed=6 * n * B, transcendentals=0),
        name="ordered",
    )(order, me, q, scale)


def local(coords, transform, labels, subject_order):
    moved = jnp.stack(
        [
            transform[:, d, 0:1] * coords[:, 0, :]
            + transform[:, d, 1:2] * coords[:, 1, :]
            + transform[:, d, 2:3] * coords[:, 2, :]
            for d in range(3)
        ]
    )
    part = jnp.pad(jnp.sum(moved, axis=2), ((0, 5), (0, 0)))
    rows = jnp.broadcast_to(labels[:, 0][None, :], (8, labels.shape[0]))
    return ordered(subject_order, lax.axis_index("subj")[None], *gram(moved, part, rows))


def solution(mesh):
    placed = (P("subj", None, "region"), P("subj", None, None), P("region", None), P())
    return jax.shard_map(
        local, mesh=mesh, in_specs=placed, out_specs=P("region", "subj", None), check_vma=False
    )
```

```python
import functools

import jax
import jax.numpy as jnp
from jax import lax
from jax.experimental import pallas as pl
from jax.experimental.pallas import tpu as pltpu
from jax.sharding import PartitionSpec as P

CAP = 256
B = 256
H = 128
G = 4
F = 3 * CAP
MESH = pl.DeviceIdType.MESH
NT = (((1,), (1,)), ((), ()))


def dev(l, c, y, z, u):
    return (2 * l + c, 8 * lax.rem(y, 4) + 2 * lax.rem(z, 4) + u)


def gram_kernel(moved, part, labels, out, out_scale, cent, parts, snd, panels, scales, res, sum_ss, sum_rs, relay_ss, relay_rs, ring_ss, ring_rs, sib_ss, sib_rs, res_ss, res_rs, scale_ss, scale_rs):
    r, s = lax.axis_index("region"), lax.axis_index("subj")
    l, c = r // 2, lax.rem(r, 2)
    y, z, u = s // 8, lax.rem(s // 2, 4), lax.rem(s, 2)
    barrier = pltpu.get_barrier_semaphore()
    own = c == u

    def copy(src, dst, ss, rs, to):
        return pltpu.make_async_remote_copy(
            src_ref=src, dst_ref=dst, send_sem=ss, recv_sem=rs, device_id=to, device_id_type=MESH
        )

    for k in range(1, 8):
        q = lax.rem(l * 4 + c * 2 + u + k, 8)
        pl.semaphore_signal(barrier, inc=1, device_id=dev(q // 4, lax.rem(q // 2, 2), y, z, lax.rem(q, 2)), device_id_type=MESH)
    for k in range(1, 4):
        for cc in range(2):
            for uu in range(2):
                pl.semaphore_signal(barrier, inc=1, device_id=dev(l, cc, y + k, z, uu), device_id_type=MESH)
                pl.semaphore_signal(barrier, inc=1, device_id=dev(l, cc, y, z + k, uu), device_id_type=MESH)
    lab = labels[...].astype(jnp.float32)[0:1, :]
    n = lab.shape[1]
    same = jnp.broadcast_to(lab, (128, n)).T[:, 0:1] == lab
    before = lax.broadcasted_iota(jnp.int32, (n, n), 0) < lax.broadcasted_iota(jnp.int32, (n, n), 1)
    rank = jnp.sum(jnp.where(jnp.logical_and(same, before), 1.0, 0.0), axis=0, keepdims=True)
    row = (lab * CAP + rank).astype(jnp.int32)
    pl.semaphore_wait(barrier, 31)

    def sums(k, owner):
        return copy(part, parts.at[owner], sum_ss.at[k - 1], sum_rs.at[owner], (lax.rem(r + k, G), s))

    for k in range(1, G):
        sums(k, r).start()
    parts[r] = part[...]
    for k in range(1, G):
        sums(k, lax.rem(r + k, G)).wait_recv()
    mean = (parts[0] + parts[1] + parts[2] + parts[3]) * (1.0 / (G * moved.shape[2]))
    for d in range(3):
        column = jnp.broadcast_to(mean[d : d + 1], (128, B)).T
        cent[d] = (moved[d] - jnp.concatenate([column] * (moved.shape[2] // 128), axis=1)).astype(jnp.bfloat16)

    def relay(half, region):
        lr, ur = region // 2, region % 2
        mine = jnp.logical_and(own, jnp.logical_and(l == lr, u == ur))
        src, dst, rs = snd.at[half, region], panels.at[r, 0, half], relay_rs.at[half, r]
        return mine, src, dst, rs, copy(src, dst, relay_ss.at[half, region], rs, dev(lr, u, y, z, ur))

    slots = lax.broadcasted_iota(jnp.int32, (CAP, row.shape[1]), 0)
    for half in range(2):
        for region in range(G):
            pick = jnp.where(slots + region * CAP == row, 1.0, 0.0).astype(jnp.bfloat16)
            found = lax.dot_general(
                cent[:, half * H : (half + 1) * H, :].reshape(3 * H, -1), pick, NT, preferred_element_type=jnp.float32
            ).astype(jnp.bfloat16)
            for d in range(3):
                snd[half, region, :, d * CAP : (d + 1) * CAP] = found[d * H : (d + 1) * H]
            mine, src, dst, rs, remote = relay(half, region)

            @pl.when(mine)
            def _():
                pltpu.make_async_copy(src, dst, rs).start()

            @pl.when(jnp.logical_not(mine))
            def _():
                remote.start()

    sibling = dev(l, 1 - c, y, z, u)
    yp, ym = dev(l, c, y + 1, z, u), dev(l, c, y + 3, z, u)
    zp, zm = dev(l, c, y, z + 1, u), dev(l, c, y, z + 3, u)

    def piece(slot, half, g):
        return scales.at[half, slot] if isinstance(g, int) and g == G else panels.at[g, slot, half]

    def place(slot):
        dy, dz = {2: 1, 4: 3, 6: 2}.get(slot // 2 * 2, 0), {8: 1, 9: 3, 10: 2}.get(slot, 0)
        return (y + (dy if slot < 8 else 0), z + dz, c if slot >= 8 or slot % 2 == 0 else 1 - c)

    def send(kind, src, dst, half, g, to):
        at = (kind, half, g)
        return copy(piece(src, half, g), piece(dst, half, g), ring_ss.at[at], ring_rs.at[at], to)

    def share(pos, half, g):
        at = (pos, half, g)
        return copy(piece(2 * pos, half, g), piece(2 * pos + 1, half, g), sib_ss.at[at], sib_rs.at[at], sibling)

    def send_own(half, g):
        send(0, 0, 4, half, g, yp).start()
        send(1, 0, 2, half, g, ym).start()
        send(2, 0, 9, half, g, zp).start()
        send(3, 0, 8, half, g, zm).start()
        share(0, half, g).start()

    first = 2 * jnp.where(own, l, 1 - l)
    turn = [lax.rem(first + i, G) for i in range(G)]
    for half in range(2):
        for g in turn:
            copy(snd.at[0, 0], panels.at[g, 0, half], relay_ss.at[0, 0], relay_rs.at[half, g], sibling).wait_recv()
            send_own(half, g)
        square = jnp.zeros((H, 1), jnp.float32)
        for g in range(G):
            x = panels[g, 0, half].astype(jnp.float32)
            square += jnp.sum(x * x, axis=1, keepdims=True)
        norm = jnp.broadcast_to(jnp.sqrt(square) * (1.0 + 2.0**-7), (H, 128)).T
        scales[half, 0] = norm[0:1, :]
        send_own(half, G)

    def inverse(half, slot):
        row = scales[half, slot]
        return jnp.where(row > 0.0, 1.0 / row, 0.0)

    def products(bs, b_halves, as_, a_halves):
        def rows(g, slots, halves):
            some = slice(halves[0], halves[-1] + 1)
            return panels[g, slots, some].reshape(-1, F)

        def inverses(slots, halves):
            return [inverse(half, k) for k in range(slots.start, slots.stop) for half in halves]

        total = None
        for g in range(G):
            part = lax.dot_general(rows(g, bs, b_halves), rows(g, as_, a_halves), NT, preferred_element_type=jnp.float32)
            total = part if total is None else total + part
        across, down = inverses(as_, a_halves), inverses(bs, b_halves)
        down = [jnp.broadcast_to(v, (128, H)).T for v in down]
        return [
            [
                total[i * H : (i + 1) * H, k * H : (k + 1) * H] * down[i] * (across[k] * 32767.0) + 12582912.0 - 12582912.0
                for k in range(len(across))
            ]
            for i in range(len(down))
        ]

    blocks = {}
    late = []

    def deliver(b, hb, a, a_halves, tiles):
        number = 8 * lax.rem(place(b)[0], 4) + 2 * lax.rem(place(b)[1], 4) + place(b)[2]
        owner = dev(l, u, *place(a))
        t, b_halves = blocks.setdefault((b, a), (len(blocks), set()))
        b_halves.add(hb)
        at = (hb, pl.ds(a_halves[0], len(a_halves)))
        for ha, tile in zip(a_halves, tiles, strict=True):
            res[t, hb, ha] = tile.astype(jnp.int32).astype(jnp.int16)
        moves = [(res.at[(t, *at)], out.at[(number, *at)], res_ss.at[t], res_rs.at[number])]
        if 0 in a_halves:
            moves.append((scales.at[hb, b], out_scale.at[number, hb], scale_ss.at[t], scale_rs.at[number]))
        for src, dst, ss, rs in moves:
            remote = copy(src, dst, ss, rs, owner)
            if a == 0:

                @pl.when(own)
                def _():
                    pltpu.make_async_copy(src, dst, rs).start()

                @pl.when(jnp.logical_not(own))
                def _():
                    remote.start()
            elif a == 1 or late is None:
                remote.start()
            else:
                across = place(a)[2] != u
                pl.when(across)(remote.start)
                late.append((jnp.logical_not(across), remote))

    def release():
        for there, remote in late:
            pl.when(there)(remote.start)

    BOTH = (0, 1)

    def straight(bs, b_halves, as_, a_halves, keep=lambda b, a: True):
        out_of = products(bs, b_halves, as_, a_halves)
        n, m = len(b_halves), len(a_halves)
        for i, b in enumerate(range(bs.start, bs.stop)):
            for p, hb in enumerate(b_halves):
                for k, a in enumerate(range(as_.start, as_.stop)):
                    if keep(b, a):
                        deliver(b, hb, a, a_halves, out_of[i * n + p][k * m : (k + 1) * m])
        return out_of

    def turned(out_of, bs, b_halves, as_, a_halves, keep=lambda b, a: True):
        n, m = len(b_halves), len(a_halves)
        for k, a in enumerate(range(as_.start, as_.stop)):
            for q, ha in enumerate(a_halves):
                for i, b in enumerate(range(bs.start, bs.stop)):
                    if keep(b, a):
                        deliver(a, ha, b, b_halves, [out_of[i * n + p][k * m + q].T for p in range(n)])

    def got_share(pos, half):
        for g in range(G + 1):
            share(pos, half, g).wait_recv()

    for half in range(2):
        got_share(0, half)
    straight(slice(0, 1), BOTH, slice(0, 2), BOTH)
    for half in range(2):
        for i, g in enumerate(turn + [G]):
            up = i % 2 == 0
            send(0, 0, 4, half, g, yp).wait_recv()
            if up:
                send(4, 4, 6, half, g, yp).start()
            share(2, half, g).start()
            send(2, 0, 9, half, g, zp).wait_recv()
            if up:
                send(5, 9, 10, half, g, zp).start()
            send(1, 0, 2, half, g, ym).wait_recv()
            if not up:
                send(4, 2, 6, half, g, ym).start()
            share(1, half, g).start()
            send(3, 0, 8, half, g, zm).wait_recv()
            if not up:
                send(5, 8, 10, half, g, zm).start()
        straight(slice(8, 10), (half,), slice(0, 2), BOTH)
        got_share(1, half)
        got_share(2, half)
        straight(slice(2, 6), (half,), slice(0, 1), BOTH)
        for hb, has in (((0,), (0,)),) if half == 0 else (((1,), BOTH), ((0,), (1,))):
            cross = slice(8, 10), hb, slice(4, 6), has
            turned(straight(*cross), *cross)
    for half in range(2):
        here = (half,)
        for g in turn + [G]:
            send(4, 4, 6, half, g, yp).wait_recv()
            share(3, half, g).start()
        for g in turn + [G]:
            send(5, 9, 10, half, g, zp).wait_recv()
        if half == 1:
            release()
            late = None
        far = slice(0, 6), BOTH, slice(10, 11), here
        turned(products(*far), *far)
        got_share(3, half)
        straight(slice(6, 8), here, slice(0, 1), BOTH)
        straight(slice(6, 8), here, slice(8, 10), BOTH)
        if half == 0:
            straight(slice(10, 11), (0,), slice(6, 8), (0,))
        else:
            opposite = slice(6, 8), (1,), slice(10, 11), BOTH
            tiles = straight(*opposite)
            turned([row[:1] for row in tiles], slice(6, 8), (1,), slice(10, 11), (0,))

    for k in range(1, G):
        sums(k, r).wait_send()
    for half in range(2):
        for region in range(G):
            mine, *_, remote = relay(half, region)

            @pl.when(jnp.logical_not(mine))
            def _():
                remote.wait_send()

        for g in range(G + 1):
            for kind in range(6):
                send(kind, 0, 2, half, g, yp).wait_send()
            for pos in range(4):
                share(pos, half, g).wait_send()
    for (_, a), (t, halves) in blocks.items():
        some = pl.ds(min(halves), len(halves))

        def left(t=t, some=some):
            copy(res.at[t, some], out.at[0, some], res_ss.at[t], res_rs.at[0], sibling).wait_send()
            copy(out_scale.at[0, some], out_scale.at[0, some], scale_ss.at[t], scale_rs.at[0], sibling).wait_send()

        if a == 0:
            pl.when(jnp.logical_not(own))(left)
        else:
            left()
    for b in range(32):
        copy(res.at[0], out.at[b], res_ss.at[0], res_rs.at[b], sibling).wait_recv()
        copy(out_scale.at[b], out_scale.at[b], scale_ss.at[0], scale_rs.at[b], sibling).wait_recv()


def gram(moved, part, labels):
    dma = pltpu.SemaphoreType.DMA
    return pl.pallas_call(
        gram_kernel,
        out_shape=(
            jax.ShapeDtypeStruct((32, 2, 2, H, H), jnp.int16),
            jax.ShapeDtypeStruct((32, 2, 1, H), jnp.float32),
        ),
        in_specs=[pl.BlockSpec(memory_space=pltpu.VMEM)] * 3,
        out_specs=[pl.BlockSpec(memory_space=pl.ANY)] * 2,
        scratch_shapes=[
            pltpu.VMEM(moved.shape, jnp.bfloat16),
            pltpu.VMEM((G, 8, B), jnp.float32),
            pltpu.VMEM((2, G, H, F), jnp.bfloat16),
            pltpu.VMEM((G, 11, 2, H, F), jnp.bfloat16),
            pltpu.VMEM((2, 11, 1, H), jnp.float32),
            pltpu.VMEM((34, 2, 2, H, H), jnp.int16),
            dma((G - 1,)),
            dma((G,)),
            dma((2, G)),
            dma((2, G)),
            dma((6, 2, G + 1)),
            dma((6, 2, G + 1)),
            dma((4, 2, G + 1)),
            dma((4, 2, G + 1)),
            dma((34,)),
            dma((32,)),
            dma((34,)),
            dma((32,)),
        ],
        compiler_params=pltpu.CompilerParams(
            collective_id=0, has_side_effects=True, vmem_limit_bytes=50 * 2**20
        ),
        cost_estimate=pl.CostEstimate(flops=13 * 10**9, bytes_accessed=10 * 2**20, transcendentals=0),
        name="gram",
    )(moved, part, labels)


W = 1024
T = 128
U = 16


def order_kernel(order, me, q_hbm, scale, out, q, table, even, odd, sems):
    step = pl.program_id(0)

    @pl.when(step == 0)
    def _():
        def scale_row(b, half):
            return scale[b, half]

        row = [scale_row(me[0], half) * (1.0 / (32767.0 * 3.0 * 2048.0)) for half in range(2)]

        def decode(b, _):
            for hb in range(2):
                column = jnp.broadcast_to(scale_row(b, hb), (128, H)).T
                for ha in range(2):
                    values = q[b, hb, ha].astype(jnp.int32).astype(jnp.float32)
                    table[pl.ds(b * 2 * B + hb * 2 * H + ha, H, stride=2), :] = values * column * row[ha]
            return 0

        def fetch(k):
            some = pl.ds(k * 4, 4)
            return pltpu.make_async_copy(q_hbm.at[some], q.at[some], sems.at[k])

        for k in range(8):
            fetch(k).start()
        for k in range(8):
            fetch(k).wait()
            lax.fori_loop(4 * k, 4 * k + 4, decode, 0)

    def gather(rows, t):
        for k in range(0, T, U):
            at = step * W + t * T + k
            loaded = [table[pl.ds(pl.multiple_of(2 * order[at + i], 2), 2), :] for i in range(U)]
            for i in range(U):
                rows[pl.ds(2 * (k + i), 2), :] = loaded[i]

    def flip(rows, t):
        for i in range(2):
            out[0, 128 * i : 128 * (i + 1), t * T : (t + 1) * T] = rows[pl.ds(i, T, stride=2), :].T

    both = (even, odd)
    gather(even, 0)
    for t in range(1, W // T):
        flip(both[(t - 1) % 2], t - 1)
        gather(both[t % 2], t)
    flip(both[(W // T - 1) % 2], W // T - 1)


def ordered(order, me, q, scale):
    n = order.shape[0]
    return pl.pallas_call(
        order_kernel,
        out_shape=jax.ShapeDtypeStruct((1, B, n), jnp.float32),
        grid_spec=pltpu.PrefetchScalarGridSpec(
            num_scalar_prefetch=2,
            grid=(n // W,),
            in_specs=[
                pl.BlockSpec(memory_space=pl.ANY),
                pl.BlockSpec(scale.shape, lambda i, o, m: (0, 0, 0, 0), pipeline_mode=pl.Buffered(1)),
            ],
            out_specs=pl.BlockSpec((1, B, W), lambda i, o, m: (0, 0, i)),
            scratch_shapes=[
                pltpu.VMEM(q.shape, q.dtype),
                pltpu.VMEM((2 * n, 128), jnp.float32),
                pltpu.VMEM((2 * T, 128), jnp.float32),
                pltpu.VMEM((2 * T, 128), jnp.float32),
                pltpu.SemaphoreType.DMA((8,)),
            ],
        ),
        compiler_params=pltpu.CompilerParams(vmem_limit_bytes=58 * 2**20),
        cost_estimate=pl.CostEstimate(flops=0, bytes_accessed=6 * n * B, transcendentals=0),
        name="ordered",
    )(order, me, q, scale)


def local(coords, transform, labels, subject_order):
    moved = jnp.stack(
        [
            transform[:, d, 0:1] * coords[:, 0, :]
            + transform[:, d, 1:2] * coords[:, 1, :]
            + transform[:, d, 2:3] * coords[:, 2, :]
            for d in range(3)
        ]
    )
    part = jnp.pad(jnp.sum(moved, axis=2), ((0, 5), (0, 0)))
    rows = jnp.broadcast_to(labels[:, 0][None, :], (8, labels.shape[0]))
    return ordered(subject_order, lax.axis_index("subj")[None], *gram(moved, part, rows))


def solution(mesh):
    placed = (P("subj", None, "region"), P("subj", None, None), P("region", None), P())
    return jax.shard_map(
        local, mesh=mesh, in_specs=placed, out_specs=P("region", "subj", None), check_vma=False
    )
```

```python
import functools

import jax
import jax.numpy as jnp
from jax import lax
from jax.experimental import pallas as pl
from jax.experimental.pallas import tpu as pltpu
from jax.sharding import PartitionSpec as P

CAP = 256
B = 256
H = 128
G = 4
F = 3 * CAP
MESH = pl.DeviceIdType.MESH
NT = (((1,), (1,)), ((), ()))


def dev(l, c, y, z, u):
    return (2 * l + c, 8 * lax.rem(y, 4) + 2 * lax.rem(z, 4) + u)


def gram_kernel(moved, part, labels, out, out_scale, cent, parts, snd, panels, scales, res, sum_ss, sum_rs, relay_ss, relay_rs, ring_ss, ring_rs, sib_ss, sib_rs, res_ss, res_rs, scale_ss, scale_rs):
    r, s = lax.axis_index("region"), lax.axis_index("subj")
    l, c = r // 2, lax.rem(r, 2)
    y, z, u = s // 8, lax.rem(s // 2, 4), lax.rem(s, 2)
    barrier = pltpu.get_barrier_semaphore()
    own = c == u

    def copy(src, dst, ss, rs, to):
        return pltpu.make_async_remote_copy(
            src_ref=src, dst_ref=dst, send_sem=ss, recv_sem=rs, device_id=to, device_id_type=MESH
        )

    for k in range(1, 8):
        q = lax.rem(l * 4 + c * 2 + u + k, 8)
        pl.semaphore_signal(barrier, inc=1, device_id=dev(q // 4, lax.rem(q // 2, 2), y, z, lax.rem(q, 2)), device_id_type=MESH)
    for k in range(1, 4):
        for cc in range(2):
            for uu in range(2):
                pl.semaphore_signal(barrier, inc=1, device_id=dev(l, cc, y + k, z, uu), device_id_type=MESH)
                pl.semaphore_signal(barrier, inc=1, device_id=dev(l, cc, y, z + k, uu), device_id_type=MESH)
    lab = labels[...].astype(jnp.float32)[0:1, :]
    n = lab.shape[1]
    same = jnp.broadcast_to(lab, (128, n)).T[:, 0:1] == lab
    before = lax.broadcasted_iota(jnp.int32, (n, n), 0) < lax.broadcasted_iota(jnp.int32, (n, n), 1)
    rank = jnp.sum(jnp.where(jnp.logical_and(same, before), 1.0, 0.0), axis=0, keepdims=True)
    row = (lab * CAP + rank).astype(jnp.int32)
    pl.semaphore_wait(barrier, 31)

    def sums(k, owner):
        return copy(part, parts.at[owner], sum_ss.at[k - 1], sum_rs.at[owner], (lax.rem(r + k, G), s))

    for k in range(1, G):
        sums(k, r).start()
    parts[r] = part[...]
    for k in range(1, G):
        sums(k, lax.rem(r + k, G)).wait_recv()
    mean = (parts[0] + parts[1] + parts[2] + parts[3]) * (1.0 / (G * moved.shape[2]))
    for d in range(3):
        column = jnp.broadcast_to(mean[d : d + 1], (128, B)).T
        cent[d] = (moved[d] - jnp.concatenate([column] * (moved.shape[2] // 128), axis=1)).astype(jnp.bfloat16)

    def relay(half, i):
        lr, ur = 1 - l if i in (1, 2) else l, 1 - u if i in (2, 3) else u
        src, dst, rs = snd.at[half, i], panels.at[r, 0, half], relay_rs.at[half, r]
        return 2 * lr + ur, src, dst, rs, copy(src, dst, relay_ss.at[half, i], rs, dev(lr, u, y, z, ur))

    slots = lax.broadcasted_iota(jnp.int32, (CAP, row.shape[1]), 0)
    for half in range(2):
        for i in range(G):
            region, src, dst, rs, remote = relay(half, i)
            pick = jnp.where(slots + region * CAP == row, 1.0, 0.0).astype(jnp.bfloat16)
            found = lax.dot_general(
                cent[:, half * H : (half + 1) * H, :].reshape(3 * H, -1), pick, NT, preferred_element_type=jnp.float32
            ).astype(jnp.bfloat16)
            for d in range(3):
                snd[half, i, :, d * CAP : (d + 1) * CAP] = found[d * H : (d + 1) * H]
            if i == 0:

                @pl.when(own)
                def _():
                    pltpu.make_async_copy(src, dst, rs).start()

                @pl.when(jnp.logical_not(own))
                def _():
                    remote.start()
            else:
                remote.start()

    sibling = dev(l, 1 - c, y, z, u)
    yp, ym = dev(l, c, y + 1, z, u), dev(l, c, y + 3, z, u)
    zp, zm = dev(l, c, y, z + 1, u), dev(l, c, y, z + 3, u)

    def piece(slot, half, g):
        return scales.at[half, slot] if isinstance(g, int) and g == G else panels.at[g, slot, half]

    def place(slot):
        dy, dz = {2: 1, 4: 3, 6: 2}.get(slot // 2 * 2, 0), {8: 1, 9: 3, 10: 2}.get(slot, 0)
        return (y + (dy if slot < 8 else 0), z + dz, c if slot >= 8 or slot % 2 == 0 else 1 - c)

    def send(kind, src, dst, half, g, to):
        at = (kind, half, g)
        return copy(piece(src, half, g), piece(dst, half, g), ring_ss.at[at], ring_rs.at[at], to)

    def share(pos, half, g):
        at = (pos, half, g)
        return copy(piece(2 * pos, half, g), piece(2 * pos + 1, half, g), sib_ss.at[at], sib_rs.at[at], sibling)

    def send_own(half, g):
        send(0, 0, 4, half, g, yp).start()
        send(1, 0, 2, half, g, ym).start()
        send(2, 0, 9, half, g, zp).start()
        send(3, 0, 8, half, g, zm).start()
        share(0, half, g).start()

    first = 2 * jnp.where(own, l, 1 - l)
    turn = [lax.rem(first + i, G) for i in range(G)]
    for half in range(2):
        for g in turn:
            copy(snd.at[0, 0], panels.at[g, 0, half], relay_ss.at[0, 0], relay_rs.at[half, g], sibling).wait_recv()
            send_own(half, g)
        square = jnp.zeros((H, 1), jnp.float32)
        for g in range(G):
            x = panels[g, 0, half].astype(jnp.float32)
            square += jnp.sum(x * x, axis=1, keepdims=True)
        norm = jnp.broadcast_to(jnp.sqrt(square) * (1.0 + 2.0**-7), (H, 128)).T
        scales[half, 0] = norm[0:1, :]
        send_own(half, G)

    def inverse(half, slot):
        row = scales[half, slot]
        return jnp.where(row > 0.0, 1.0 / row, 0.0)

    def products(bs, b_halves, as_, a_halves):
        def rows(g, slots, halves):
            some = slice(halves[0], halves[-1] + 1)
            return panels[g, slots, some].reshape(-1, F)

        def inverses(slots, halves):
            return [inverse(half, k) for k in range(slots.start, slots.stop) for half in halves]

        total = None
        for g in range(G):
            part = lax.dot_general(rows(g, bs, b_halves), rows(g, as_, a_halves), NT, preferred_element_type=jnp.float32)
            total = part if total is None else total + part
        across, down = inverses(as_, a_halves), inverses(bs, b_halves)
        down = [jnp.broadcast_to(v, (128, H)).T for v in down]
        return [
            [
                total[i * H : (i + 1) * H, k * H : (k + 1) * H] * down[i] * (across[k] * 32767.0) + 12582912.0 - 12582912.0
                for k in range(len(across))
            ]
            for i in range(len(down))
        ]

    blocks = {}
    late = []

    def deliver(b, hb, a, a_halves, tiles):
        number = 8 * lax.rem(place(b)[0], 4) + 2 * lax.rem(place(b)[1], 4) + place(b)[2]
        owner = dev(l, u, *place(a))
        t, b_halves = blocks.setdefault((b, a), (len(blocks), set()))
        b_halves.add(hb)
        at = (hb, pl.ds(a_halves[0], len(a_halves)))
        for ha, tile in zip(a_halves, tiles, strict=True):
            res[t, hb, ha] = tile.astype(jnp.int32).astype(jnp.int16)
        moves = [(res.at[(t, *at)], out.at[(number, *at)], res_ss.at[t], res_rs.at[number])]
        if 0 in a_halves:
            moves.append((scales.at[hb, b], out_scale.at[number, hb], scale_ss.at[t], scale_rs.at[number]))
        for src, dst, ss, rs in moves:
            remote = copy(src, dst, ss, rs, owner)
            if a == 0:

                @pl.when(own)
                def _():
                    pltpu.make_async_copy(src, dst, rs).start()

                @pl.when(jnp.logical_not(own))
                def _():
                    remote.start()
            elif a == 1 or late is None:
                remote.start()
            else:
                across = place(a)[2] != u
                pl.when(across)(remote.start)
                late.append((jnp.logical_not(across), remote))

    def release():
        for there, remote in late:
            pl.when(there)(remote.start)

    BOTH = (0, 1)

    def straight(bs, b_halves, as_, a_halves, keep=lambda b, a: True):
        out_of = products(bs, b_halves, as_, a_halves)
        n, m = len(b_halves), len(a_halves)
        for i, b in enumerate(range(bs.start, bs.stop)):
            for p, hb in enumerate(b_halves):
                for k, a in enumerate(range(as_.start, as_.stop)):
                    if keep(b, a):
                        deliver(b, hb, a, a_halves, out_of[i * n + p][k * m : (k + 1) * m])
        return out_of

    def turned(out_of, bs, b_halves, as_, a_halves, keep=lambda b, a: True):
        n, m = len(b_halves), len(a_halves)
        for k, a in enumerate(range(as_.start, as_.stop)):
            for q, ha in enumerate(a_halves):
                for i, b in enumerate(range(bs.start, bs.stop)):
                    if keep(b, a):
                        deliver(a, ha, b, b_halves, [out_of[i * n + p][k * m + q].T for p in range(n)])

    def got_share(pos, half):
        for g in range(G + 1):
            share(pos, half, g).wait_recv()

    for half in range(2):
        got_share(0, half)
    straight(slice(0, 1), BOTH, slice(0, 2), BOTH)
    for half in range(2):
        for i, g in enumerate(turn + [G]):
            up = i % 2 == 0
            send(0, 0, 4, half, g, yp).wait_recv()
            if up:
                send(4, 4, 6, half, g, yp).start()
            share(2, half, g).start()
            send(2, 0, 9, half, g, zp).wait_recv()
            if up:
                send(5, 9, 10, half, g, zp).start()
            send(1, 0, 2, half, g, ym).wait_recv()
            if not up:
                send(4, 2, 6, half, g, ym).start()
            share(1, half, g).start()
            send(3, 0, 8, half, g, zm).wait_recv()
            if not up:
                send(5, 8, 10, half, g, zm).start()
        straight(slice(8, 10), (half,), slice(0, 2), BOTH)
        got_share(1, half)
        got_share(2, half)
        straight(slice(2, 6), (half,), slice(0, 1), BOTH)
        for hb, has in (((0,), (0,)),) if half == 0 else (((1,), BOTH), ((0,), (1,))):
            cross = slice(8, 10), hb, slice(4, 6), has
            turned(straight(*cross), *cross)
    for half in range(2):
        here = (half,)
        for g in turn + [G]:
            send(4, 4, 6, half, g, yp).wait_recv()
            share(3, half, g).start()
        for g in turn + [G]:
            send(5, 9, 10, half, g, zp).wait_recv()
        if half == 1:
            release()
            late = None
        far = slice(0, 6), BOTH, slice(10, 11), here
        turned(products(*far), *far)
        got_share(3, half)
        straight(slice(6, 8), here, slice(0, 1), BOTH)
        straight(slice(6, 8), here, slice(8, 10), BOTH)
        if half == 0:
            straight(slice(10, 11), (0,), slice(6, 8), (0,))
        else:
            opposite = slice(6, 8), (1,), slice(10, 11), BOTH
            tiles = straight(*opposite)
            turned([row[:1] for row in tiles], slice(6, 8), (1,), slice(10, 11), (0,))

    for k in range(1, G):
        sums(k, r).wait_send()
    for half in range(2):
        for i in range(G):
            *_, remote = relay(half, i)
            if i == 0:
                pl.when(jnp.logical_not(own))(remote.wait_send)
            else:
                remote.wait_send()

        for g in range(G + 1):
            for kind in range(6):
                send(kind, 0, 2, half, g, yp).wait_send()
            for pos in range(4):
                share(pos, half, g).wait_send()
    for (_, a), (t, halves) in blocks.items():
        some = pl.ds(min(halves), len(halves))

        def left(t=t, some=some):
            copy(res.at[t, some], out.at[0, some], res_ss.at[t], res_rs.at[0], sibling).wait_send()
            copy(out_scale.at[0, some], out_scale.at[0, some], scale_ss.at[t], scale_rs.at[0], sibling).wait_send()

        if a == 0:
            pl.when(jnp.logical_not(own))(left)
        else:
            left()
    for b in range(32):
        copy(res.at[0], out.at[b], res_ss.at[0], res_rs.at[b], sibling).wait_recv()
        copy(out_scale.at[b], out_scale.at[b], scale_ss.at[0], scale_rs.at[b], sibling).wait_recv()


def gram(moved, part, labels):
    dma = pltpu.SemaphoreType.DMA
    return pl.pallas_call(
        gram_kernel,
        out_shape=(
            jax.ShapeDtypeStruct((32, 2, 2, H, H), jnp.int16),
            jax.ShapeDtypeStruct((32, 2, 1, H), jnp.float32),
        ),
        in_specs=[pl.BlockSpec(memory_space=pltpu.VMEM)] * 3,
        out_specs=[pl.BlockSpec(memory_space=pl.ANY)] * 2,
        scratch_shapes=[
            pltpu.VMEM(moved.shape, jnp.bfloat16),
            pltpu.VMEM((G, 8, B), jnp.float32),
            pltpu.VMEM((2, G, H, F), jnp.bfloat16),
            pltpu.VMEM((G, 11, 2, H, F), jnp.bfloat16),
            pltpu.VMEM((2, 11, 1, H), jnp.float32),
            pltpu.VMEM((34, 2, 2, H, H), jnp.int16),
            dma((G - 1,)),
            dma((G,)),
            dma((2, G)),
            dma((2, G)),
            dma((6, 2, G + 1)),
            dma((6, 2, G + 1)),
            dma((4, 2, G + 1)),
            dma((4, 2, G + 1)),
            dma((34,)),
            dma((32,)),
            dma((34,)),
            dma((32,)),
        ],
        compiler_params=pltpu.CompilerParams(
            collective_id=0, has_side_effects=True, vmem_limit_bytes=50 * 2**20
        ),
        cost_estimate=pl.CostEstimate(flops=13 * 10**9, bytes_accessed=10 * 2**20, transcendentals=0),
        name="gram",
    )(moved, part, labels)


W = 1024
T = 128
U = 16


def order_kernel(order, me, q_hbm, scale, out, q, table, even, odd, sems):
    step = pl.program_id(0)

    @pl.when(step == 0)
    def _():
        def scale_row(b, half):
            return scale[b, half]

        row = [scale_row(me[0], half) * (1.0 / (32767.0 * 3.0 * 2048.0)) for half in range(2)]

        def decode(b, _):
            for hb in range(2):
                column = jnp.broadcast_to(scale_row(b, hb), (128, H)).T
                for ha in range(2):
                    values = q[b, hb, ha].astype(jnp.int32).astype(jnp.float32)
                    table[pl.ds(b * 2 * B + hb * 2 * H + ha, H, stride=2), :] = values * column * row[ha]
            return 0

        def fetch(k):
            some = pl.ds(k * 4, 4)
            return pltpu.make_async_copy(q_hbm.at[some], q.at[some], sems.at[k])

        for k in range(8):
            fetch(k).start()
        for k in range(8):
            fetch(k).wait()
            lax.fori_loop(4 * k, 4 * k + 4, decode, 0)

    def gather(rows, t):
        for k in range(0, T, U):
            at = step * W + t * T + k
            loaded = [table[pl.ds(pl.multiple_of(2 * order[at + i], 2), 2), :] for i in range(U)]
            for i in range(U):
                rows[pl.ds(2 * (k + i), 2), :] = loaded[i]

    def flip(rows, t):
        for i in range(2):
            out[0, 128 * i : 128 * (i + 1), t * T : (t + 1) * T] = rows[pl.ds(i, T, stride=2), :].T

    both = (even, odd)
    gather(even, 0)
    for t in range(1, W // T):
        flip(both[(t - 1) % 2], t - 1)
        gather(both[t % 2], t)
    flip(both[(W // T - 1) % 2], W // T - 1)


def ordered(order, me, q, scale):
    n = order.shape[0]
    return pl.pallas_call(
        order_kernel,
        out_shape=jax.ShapeDtypeStruct((1, B, n), jnp.float32),
        grid_spec=pltpu.PrefetchScalarGridSpec(
            num_scalar_prefetch=2,
            grid=(n // W,),
            in_specs=[
                pl.BlockSpec(memory_space=pl.ANY),
                pl.BlockSpec(scale.shape, lambda i, o, m: (0, 0, 0, 0), pipeline_mode=pl.Buffered(1)),
            ],
            out_specs=pl.BlockSpec((1, B, W), lambda i, o, m: (0, 0, i)),
            scratch_shapes=[
                pltpu.VMEM(q.shape, q.dtype),
                pltpu.VMEM((2 * n, 128), jnp.float32),
                pltpu.VMEM((2 * T, 128), jnp.float32),
                pltpu.VMEM((2 * T, 128), jnp.float32),
                pltpu.SemaphoreType.DMA((8,)),
            ],
        ),
        compiler_params=pltpu.CompilerParams(vmem_limit_bytes=58 * 2**20),
        cost_estimate=pl.CostEstimate(flops=0, bytes_accessed=6 * n * B, transcendentals=0),
        name="ordered",
    )(order, me, q, scale)


def local(coords, transform, labels, subject_order):
    moved = jnp.stack(
        [
            transform[:, d, 0:1] * coords[:, 0, :]
            + transform[:, d, 1:2] * coords[:, 1, :]
            + transform[:, d, 2:3] * coords[:, 2, :]
            for d in range(3)
        ]
    )
    part = jnp.pad(jnp.sum(moved, axis=2), ((0, 5), (0, 0)))
    rows = jnp.broadcast_to(labels[:, 0][None, :], (8, labels.shape[0]))
    return ordered(subject_order, lax.axis_index("subj")[None], *gram(moved, part, rows))


def solution(mesh):
    placed = (P("subj", None, "region"), P("subj", None, None), P("region", None), P())
    return jax.shard_map(
        local, mesh=mesh, in_specs=placed, out_specs=P("region", "subj", None), check_vma=False
    )
```
